32 devices in a mesh: expert: 8 (over z, y), wshard: 4 (over x, core).
Axes of the slice: x: 2, y: 2, z: 4, core: 2. Of those that a mesh axis runs over, the one named last changes fastest.
Arguments:
- tokens: bfloat16 [16384, 768], P(('expert', 'wshard')), may hold values from -6 to 6
- attn_norm: bfloat16 [768], P('wshard'), may hold values from 0.5 to 1.5
- attn_in: bfloat16 [768, 2304], P('wshard'), may hold values from -0.21875 to 0.21875
- attn_out: bfloat16 [768, 768], P('wshard'), may hold values from -6 to 6
- rel_bias: bfloat16 [32, 12], replicated, may hold values from -6 to 6
- buckets: int32 [4095], replicated, may hold values from 0 to 31
- ffn_norm: bfloat16 [768], P('wshard'), may hold values from 0.5 to 1.5
- router: bfloat16 [768, 8], P('wshard'), may hold values from -0.375 to 0.375
- routes: int32 [16384, 1], P(('expert', 'wshard')), may hold values from 0 to 7; in each aligned block of 512 rows (0 to 511, 512 to 1023, ...) at most 128 rows name the same one
- expert_in: bfloat16 [8, 768, 3072], P('expert'), may hold values from -0.21875 to 0.21875
- expert_out: bfloat16 [8, 3072, 768], P('expert'), may hold values from -2 to 2
- cotangent: bfloat16 [16384, 768], P(('expert', 'wshard')), may hold values from -6 to 6
Outputs:
- mixed: bfloat16 [16384, 768], P(('expert', 'wshard'))
- grad_tokens: float32 [16384, 768], P(('expert', 'wshard'))
- grad_attn_norm: float32 [768], P(('expert', 'wshard'))
- grad_attn_in: float32 [768, 2304], P(('expert', 'wshard'))
- grad_attn_out: float32 [768, 768], P(('expert', 'wshard'))
- grad_rel_bias: float32 [32, 12], replicated
- grad_ffn_norm: float32 [768], P(('expert', 'wshard'))
- grad_router: float32 [768, 8], P(('expert', 'wshard'))
- grad_expert_in: float32 [8, 768, 3072], P('expert', None, 'wshard')
- grad_expert_out: float32 [8, 3072, 768], P('expert', 'wshard')
The draws below stay inside these ranges and needn't reach their ends.
Inputs may be any that keep to these rules, and one draw needn't show every extreme that they name: `routes`: among the rows of one device no expert is named by more than 128 rows, and on some device some expert is named by exactly 128.
All inputs are finite; a program needn't handle non-finite values.
Results may differ from the reference program's by a relative error of at most 0.015.
Values may be sent and summed in bfloat16 or wider, within the bound.
No kernel may reach another device: no remote copies, remote signals or barrier semaphores. Data moves between devices by JAX's collectives and lax.ppermute only.
A program may use at most 256 MiB of HBM per device.

```python
import math
from functools import partial
import jax
import jax.numpy as jnp
import numpy as np
from jax import lax

D = 768
HEADS = 12
HD = 64
FF = 3072
NB = 32
EXPERTS = 8
TOK_DEV = 512
SEQ = 2048
CAP = 128
TOKENS = 16384
N_EXPERT = 8
N_WSHARD = 4


def place_ends(entries, rng, smallest, largest):
    longest = entries.shape.index(max(entries.shape))
    spots = []
    for shift in (0, 1):
        where = [jax.random.randint(jax.random.fold_in(rng, axis), (), 0, length) for axis, length in enumerate(entries.shape)]
        where[longest] = (where[longest] + shift) % entries.shape[longest]
        spots.append(tuple(where))
    return entries.at[spots[0]].set(smallest).at[spots[1]].set(largest)


def block_scale(stream_key, dims, shards, least, high):
    loudness = 1.0
    for dim, parts in shards:
        draws = jax.random.uniform(jax.random.fold_in(jax.random.fold_in(stream_key, 6), dim), (parts,), jnp.float32, least / len(shards), high / len(shards))
        loudness = loudness * jnp.repeat(jnp.exp(draws), dims[dim] // parts).reshape((-1,) + (1,) * (len(dims) - 1 - dim))
    return loudness


def assign_block(stream_key, own, number, rows, amount, top, reach, slope):
    ranking = jax.random.permutation(stream_key, amount)
    crowded, ordinary = shares(amount, rows * top, reach, slope, True), shares(amount, rows * top, reach, slope, False)
    places = jnp.arange(amount)

    def named(tallies, rotation):
        used = int((tallies > 0).sum())
        fixed = max(1, used // 4)
        moved = fixed + (places - fixed + rotation * (used - fixed)) % max(1, amount - fixed)
        return jnp.zeros((amount,), jnp.int32).at[ranking[jnp.where(places < fixed, places, moved)]].set(jnp.asarray(tallies, jnp.int32))

    tallies = jnp.where(number % 4 == 0, named(crowded, number // 4), named(ordinary, number - number // 4 - 1))
    mixed = jax.random.permutation(jax.random.fold_in(own, 3), amount)
    giver, taker = mixed[0:amount // 2 * 2:2], mixed[1:amount // 2 * 2:2]
    room = jnp.minimum(tallies[giver] - 1, reach - tallies[taker]) // 2
    room = jnp.where((giver == ranking[0]) | (taker == ranking[0]) | (tallies[taker] == 0), 0, jnp.maximum(room, 0))
    moved = jax.random.randint(jax.random.fold_in(own, 4), (amount // 2,), 0, 1 << 20) % (room + 1)
    tallies = tallies.at[giver].add(-moved).at[taker].add(moved)
    items = jnp.searchsorted(jnp.cumsum(tallies), jnp.arange(rows * top), side="right").astype(jnp.int32)
    table = items.reshape(top, rows).T
    table = table[jax.random.permutation(jax.random.fold_in(own, 1), rows)]
    rotation = jax.random.randint(jax.random.fold_in(own, 2), (rows, 1), 0, top)
    return jnp.take_along_axis(table, (jnp.arange(top)[None, :] + rotation) % top, axis=1)


def shares(number_of, total, reach, slope, full):
    portions = [(1 << 20) // math.isqrt(standing ** slope) + 1 for standing in range(1, number_of + 1)]
    largest = reach if full else min(reach, max(-(-total // number_of), total * portions[0] // sum(portions)))
    least = 1 if total - largest >= number_of - 1 else 0
    given, rest = [largest] + [least] * (number_of - 1), total - largest - least * (number_of - 1)
    while rest > 0:
        candidates = [i for i in range(1, number_of) if given[i] < largest] or [i for i in range(1, number_of) if given[i] < reach]
        mass, remaining = sum([portions[i] for i in candidates]), rest
        for i in candidates:
            addition = min(reach - given[i], max(1, remaining * portions[i] // mass), rest)
            given[i] = given[i] + addition
            rest = rest - addition
    return np.array(given)


def normal_values(key, extent, spread, bound, pieces=(), held_as=jnp.bfloat16):
    gain = block_scale(key, extent, pieces, -0.22, 0.18) if pieces else 1.0
    drawn = jax.random.normal(key, extent, jnp.float32) * spread * gain
    return jnp.minimum(jnp.maximum(drawn, -bound), bound).astype(held_as)


def setup_inputs(seed: int = 0) -> dict:
    key_of = jax.random.split(jax.random.key(seed), 13)
    tokens = normal_values(key_of[0], (TOKENS, D), 1.0, 6.0, ((0, 32),))
    attn_norm = jnp.clip(1.0 + 0.1 * jax.random.normal(key_of[1], (D,), jnp.float32), 0.5, 1.5).astype(jnp.bfloat16)
    attn_in = normal_values(key_of[2], (D, 3 * D), D ** -0.5, 0.21875, ((0, 4),))
    attn_out = normal_values(key_of[3], (D, D), (0.4 * SEQ ** 0.5 * D ** -0.5), 6.0, ((0, 4),))
    rel_bias = normal_values(key_of[4], (NB, HEADS), 1.0, 6.0)
    buckets = place_ends(jax.random.randint(key_of[5], (2 * SEQ - 1,), 0, NB), jax.random.fold_in(key_of[5], 1), 0, NB - 1).astype(jnp.int32)
    ffn_norm = jnp.clip(1.0 + 0.1 * jax.random.normal(key_of[6], (D,), jnp.float32), 0.5, 1.5).astype(jnp.bfloat16)
    router = normal_values(key_of[7], (D, EXPERTS), (0.75 * D ** -0.5), 0.375, ((0, 4),))
    routes_keys = jax.random.split(jax.random.fold_in(key_of[8], 1), TOKENS // TOK_DEV)
    routes_turns = jax.random.permutation(jax.random.fold_in(key_of[8], 3), TOKENS // TOK_DEV)
    routes = jax.vmap(lambda own, number: assign_block(jax.random.fold_in(key_of[8], 2), own, number, TOK_DEV, EXPERTS, 1, CAP, 1))(routes_keys, routes_turns).reshape((TOKENS, 1))
    expert_in = normal_values(key_of[9], (EXPERTS, D, FF), D ** -0.5, 0.21875, ((0, 8),))
    expert_out = normal_values(key_of[10], (EXPERTS, FF, D), (EXPERTS * FF ** -0.5), 2.0, ((0, 8),))
    cotangent = normal_values(key_of[11], (TOKENS, D), 1.0, 6.0, ((0, 32),))
    return {"tokens": tokens, "attn_norm": attn_norm, "attn_in": attn_in, "attn_out": attn_out, "rel_bias": rel_bias, "buckets": buckets, "ffn_norm": ffn_norm, "router": router, "routes": routes, "expert_in": expert_in, "expert_out": expert_out, "cotangent": cotangent}


epsilon = 1e-06
highest = lax.Precision.HIGHEST

@jax.custom_vjp
def low(v):
    return lax.optimization_barrier(v.astype(jnp.bfloat16)).astype(jnp.float32)

@jax.custom_vjp
def low_back(v):
    return v

def low_keep(v):
    return (low(v), None)

def low_pass(kept, grad):
    return (grad,)

def back_keep(v):
    return (v, None)

def back_low(kept, grad):
    return (low(grad),)
low.defvjp(low_keep, low_pass)
low_back.defvjp(back_keep, back_low)

def rms_scale(values):
    return lax.rsqrt(lax.optimization_barrier(jnp.mean(values * values, axis=-1, keepdims=True)) + epsilon)

def attention_group(bias_grid, qkv_rows):
    group_count = qkv_rows.shape[0] // SEQ
    split_rows = qkv_rows.reshape(group_count, SEQ, 3, HEADS, HD)
    scores = low_back(jnp.einsum('gqhd,gkhd->ghqk', split_rows[:, :, 0], split_rows[:, :, 1], precision=highest) * 0.125)
    scores = scores + bias_grid[None]
    shifted = jnp.exp(scores - lax.optimization_barrier(jnp.max(scores, axis=-1, keepdims=True)))
    weights = low(shifted / lax.optimization_barrier(jnp.sum(shifted, axis=-1, keepdims=True)))
    mixed_heads = jnp.einsum('ghqk,gkhd->gqhd', weights, split_rows[:, :, 2], precision=highest)
    return mixed_heads.reshape(group_count * SEQ, D)

def expert_apply(items):
    expert_rows, weight_in, weight_out = items
    inner_act = low_back(jnp.dot(expert_rows, weight_in, precision=highest))
    hidden_act = low(jax.nn.gelu(inner_act))
    return jnp.dot(hidden_act, weight_out, precision=highest)

def reference(tokens, attn_norm, attn_in, attn_out, rel_bias, buckets, ffn_norm, router, routes, expert_in, expert_out, cotangent):
    device_count = N_EXPERT * N_WSHARD
    route_ids = routes[:, 0]
    positions = jnp.arange(SEQ, dtype=jnp.int32)
    bucket_grid = buckets[positions[None, :] - positions[:, None] + SEQ - 1]
    per_device = route_ids.reshape(device_count, TOK_DEV)
    device_hot = (per_device[:, :, None] == jnp.arange(EXPERTS, dtype=jnp.int32)[None, None, :]).astype(jnp.int32)
    slot_rank = lax.optimization_barrier(jnp.sum((jnp.cumsum(device_hot, axis=1) - 1) * device_hot, axis=2))
    owners = jnp.arange(device_count, dtype=jnp.int32)[:, None]
    slot_index = (per_device * (device_count * CAP) + owners * CAP + slot_rank).reshape(-1).astype(jnp.int32)
    route_hot = (route_ids[:, None] == jnp.arange(EXPERTS, dtype=jnp.int32)[None, :]).astype(jnp.float32)
    group_count = math.gcd(max(1, 4096 // SEQ), TOKENS // SEQ)

    def forward(start, gain_a, weight_qkv, weight_o, bias_table, gain_f, weight_router, weight_in, weight_out):
        normed = low(start * rms_scale(start) * gain_a)
        qkv = low_back(low(jnp.dot(normed, weight_qkv, precision=highest)))
        bias_grid = jnp.transpose(bias_table[bucket_grid], (2, 0, 1))
        grouped = qkv.reshape(-1, group_count * SEQ, 3 * D)
        mixed_heads = lax.map(jax.checkpoint(partial(attention_group, bias_grid)), grouped)
        mixed_heads = low_back(low(mixed_heads.reshape(-1, D)))
        branch = low_back(jnp.dot(mixed_heads, weight_o, precision=highest))
        middle = start + branch
        normed_f = low(middle * rms_scale(middle) * gain_f)
        logits = low_back(jnp.dot(normed_f, weight_router, precision=highest))
        shifted = jnp.exp(logits - lax.optimization_barrier(jnp.max(logits, axis=-1, keepdims=True)))
        router_probs = shifted / lax.optimization_barrier(jnp.sum(shifted, axis=-1, keepdims=True))
        gate_prob = lax.optimization_barrier(jnp.sum(router_probs * route_hot, axis=-1, keepdims=True))
        sent_rows = low_back(normed_f)
        slots_all = jnp.zeros((EXPERTS * device_count * CAP, D), jnp.float32).at[slot_index].set(sent_rows)
        results = lax.map(jax.checkpoint(expert_apply), (slots_all.reshape(EXPERTS, device_count * CAP, D), weight_in, weight_out))
        expert_result = low_back(low(results.reshape(-1, D)[slot_index]))
        return middle + gate_prob * expert_result
    output, pullback = jax.vjp(forward, tokens.astype(jnp.float32), attn_norm.astype(jnp.float32), attn_in.astype(jnp.float32), attn_out.astype(jnp.float32), rel_bias.astype(jnp.float32), ffn_norm.astype(jnp.float32), router.astype(jnp.float32), expert_in.astype(jnp.float32), expert_out.astype(jnp.float32))
    grads = pullback(cotangent.astype(jnp.float32))
    return (output.astype(jnp.bfloat16), grads[0], grads[1], grads[2], grads[3], grads[4], grads[5], grads[6], grads[7], grads[8])
```

```python
import functools
import math

import jax
import jax.numpy as jnp
from jax import lax
from jax.experimental import pallas as pl
from jax.experimental.pallas import tpu as pltpu
from jax.sharding import PartitionSpec as P

epsilon = 1e-06
highest = lax.Precision.HIGHEST
f32 = jnp.float32
bf16 = jnp.bfloat16
LOG2E = math.log2(math.e)
LANES = 128
BLOCK = 256


def rms_scale(values):
    return lax.rsqrt(jnp.mean(values * values, axis=-1, keepdims=True) + epsilon)


def norm_back(grad_normed, values, scale, gain):
    scaled = grad_normed * gain
    inner_mean = jnp.mean(scaled * values, axis=-1, keepdims=True)
    grad_values = scale * scaled - values * (scale * scale * scale) * inner_mean
    return (grad_values, jnp.sum(grad_normed * values * scale, axis=0))


def build_bias(offsets, bias_ref):
    chunks = offsets.shape[0]
    rows = jnp.broadcast_to(offsets[:, None, :], (chunks, 8, LANES)).reshape(chunks * 8, LANES)
    sub = lax.broadcasted_iota(jnp.int32, (chunks * 8, LANES), 0) % 8
    for bit in (1, 2, 4):
        rows = jnp.where((sub & bit) != 0, pltpu.roll(rows, bit, 1), rows)
    lane = lax.broadcasted_iota(jnp.int32, (8, LANES), 1)
    sub8 = lax.broadcasted_iota(jnp.int32, (8, LANES), 0)
    for part in range(LANES // 8):
        turned = pltpu.roll(rows, 8 * part, 1) if part else rows
        upper = lane >= sub8 + 8 * part
        for tile in range(chunks - 1):
            chunk = chunks - 1 - tile
            bias_ref[tile * LANES + 8 * part : tile * LANES + 8 * part + 8, :] = jnp.where(
                upper, turned[chunk * 8 : chunk * 8 + 8], turned[chunk * 8 - 8 : chunk * 8]
            )


def fold_bias(grad_ref, chunks):
    lane = lax.broadcasted_iota(jnp.int32, (LANES, LANES), 1)
    sub = lax.broadcasted_iota(jnp.int32, (LANES, LANES), 0)
    upper = lane >= sub
    pieces = []
    for chunk in range(chunks):
        total = None
        if chunk >= 1:
            start = (chunks - 1 - chunk) * LANES
            total = jnp.where(upper, grad_ref[start : start + LANES, :], 0.0)
        if chunk <= chunks - 2:
            start = (chunks - 2 - chunk) * LANES
            lower = jnp.where(upper, 0.0, grad_ref[start : start + LANES, :])
            total = lower if total is None else total + lower
        half = LANES // 2
        while half >= 8:
            total = total[:half] + pltpu.roll(total[half:], LANES - half, 1)
            half //= 2
        pieces.append(total)
    stacked = jnp.concatenate(pieces, axis=0)
    sub8 = lax.broadcasted_iota(jnp.int32, (chunks * 8, LANES), 0) % 8
    for bit in (1, 2, 4):
        stacked = jnp.where((sub8 & bit) != 0, pltpu.roll(stacked, LANES - bit, 1), stacked)
    return jnp.sum(stacked.reshape(chunks, 8, LANES), axis=1)


def split_scaled(query):
    scaled = query.astype(f32) * (0.125 * LOG2E)
    high = scaled.astype(bf16)
    low = (scaled - high.astype(f32)).astype(bf16)
    return jnp.concatenate([high, low], axis=0)


def strips(bias_ref, tiles, first, start, count):
    parts = []
    for index in range(count):
        row = (tiles - 1 - (first + index)) * LANES + start
        parts.append(bias_ref[pl.ds(pl.multiple_of(row, LANES), BLOCK), :])
    return jnp.concatenate(parts, axis=1)


def forward_kernel(
    offset_ref, query_ref, key_ref, value_ref, mixed_ref, log_ref, bias_ref, key2_ref, value_aug_ref, score_ref
):
    size, length = query_ref.shape
    tiles = length // LANES
    blocks = length // BLOCK
    across = BLOCK // LANES
    build_bias(offset_ref[0] * LOG2E, bias_ref)
    keys = key_ref[...].astype(f32).T.astype(bf16)
    key2_ref[...] = jnp.concatenate([keys, keys], axis=1)
    value_aug_ref[:size, :] = value_ref[...]
    extra = lax.broadcasted_iota(jnp.int32, (16, length), 0)
    value_aug_ref[size:, :] = jnp.where(extra == 0, 1.0, 0.0).astype(bf16)

    def one_block(block, carry):
        columns = pl.ds(pl.multiple_of(block * BLOCK, BLOCK), BLOCK)
        query2 = split_scaled(query_ref[:, columns])
        top = jnp.full((1, BLOCK), -jnp.inf, f32)
        for chunk in range(blocks):
            start = chunk * BLOCK
            scores = jnp.dot(key2_ref[start : start + BLOCK, :], query2, preferred_element_type=f32)
            scores = scores + strips(bias_ref, tiles, block * across, start, across)
            score_ref[start : start + BLOCK, :] = scores
            top = jnp.maximum(top, jnp.max(scores, axis=0, keepdims=True))
        total = jnp.zeros((size + 16, BLOCK), f32)
        for chunk in range(blocks):
            start = chunk * BLOCK
            weights = jnp.exp2(score_ref[start : start + BLOCK, :] - top).astype(bf16)
            total = total + jnp.dot(
                value_aug_ref[:, start : start + BLOCK], weights, preferred_element_type=f32
            )
        row_total = total[size : size + 1]
        mixed_ref[:, columns] = (total[:size] / row_total).astype(bf16)
        log_ref[0, :, columns] = top + jnp.log2(row_total)
        return carry

    lax.fori_loop(0, blocks, one_block, 0)


def backward_kernel(
    offset_ref,
    query_ref,
    key_ref,
    value_ref,
    grad_ref,
    mixed_ref,
    log_ref,
    dquery_ref,
    dkey_ref,
    dvalue_ref,
    doffset_ref,
    bias_ref,
    dbias_ref,
    query2_ref,
    query_rows_ref,
    grad_rows_ref,
    key2_ref,
    value_rows_ref,
    delta_ref,
    weight_ref,
    score_ref,
    dquery_acc_ref,
):
    size, length = query_ref.shape
    tiles = length // LANES
    blocks = length // BLOCK
    across = BLOCK // LANES
    build_bias(offset_ref[0] * LOG2E, bias_ref)
    dbias_ref[...] = jnp.zeros_like(dbias_ref)
    query2_ref[...] = split_scaled(query_ref[...])
    query_rows_ref[...] = query_ref[...].astype(f32).T.astype(bf16)
    grad = grad_ref[...].astype(f32)
    grad_rows_ref[...] = grad.T.astype(bf16)
    keys = key_ref[...].astype(f32).T.astype(bf16)
    key2_ref[...] = jnp.concatenate([keys, keys], axis=1)
    value_rows_ref[...] = value_ref[...].astype(f32).T.astype(bf16)
    delta_ref[...] = jnp.sum(grad * mixed_ref[...].astype(f32), axis=0, keepdims=True)
    dquery_acc_ref[...] = jnp.zeros_like(dquery_acc_ref)

    def one_chunk(chunk, carry):
        start = pl.multiple_of(chunk * BLOCK, BLOCK)
        rows = pl.ds(start, BLOCK)
        for block in range(blocks):
            columns = slice(block * BLOCK, (block + 1) * BLOCK)
            scores = jnp.dot(key2_ref[rows, :], query2_ref[:, columns], preferred_element_type=f32)
            scores = scores + strips(bias_ref, tiles, block * across, start, across)
            weights = jnp.exp2(scores - log_ref[0, :, columns])
            weight_ref[:, columns] = weights.astype(bf16)
            dweights = jnp.dot(value_rows_ref[rows, :], grad_ref[:, columns], preferred_element_type=f32)
            dscores = weights * (dweights - delta_ref[:, columns])
            for index in range(across):
                row = (tiles - 1 - (block * across + index)) * LANES + start
                place = pl.ds(pl.multiple_of(row, LANES), BLOCK)
                dbias_ref[place, :] += dscores[:, index * LANES : (index + 1) * LANES]
            low = dscores.astype(bf16)
            score_ref[:, columns] = low
            dquery_acc_ref[:, columns] += jnp.dot(key_ref[:, rows], low, preferred_element_type=f32)
        dvalue = jnp.dot(weight_ref[...], grad_rows_ref[...], preferred_element_type=f32)
        dkey = jnp.dot(score_ref[...], query_rows_ref[...], preferred_element_type=f32) * 0.125
        dvalue_ref[:, rows] = dvalue.T.astype(bf16)
        dkey_ref[:, rows] = dkey.T.astype(bf16)
        return carry

    lax.fori_loop(0, blocks, one_chunk, 0)
    dquery_ref[...] = (dquery_acc_ref[...] * 0.125).astype(bf16)
    doffset_ref[0] = fold_bias(dbias_ref, offset_ref.shape[1])


def attention_forward(offsets, qkv, heads):
    columns, length = qkv.shape
    size = columns // (3 * heads)
    chunks = offsets.shape[1]
    elements = heads * length * length
    return pl.pallas_call(
        forward_kernel,
        grid=(heads,),
        in_specs=[
            pl.BlockSpec((1, chunks, LANES), lambda h: (h, 0, 0)),
            pl.BlockSpec((size, length), lambda h: (h, 0)),
            pl.BlockSpec((size, length), lambda h: (heads + h, 0)),
            pl.BlockSpec((size, length), lambda h: (2 * heads + h, 0)),
        ],
        out_specs=[
            pl.BlockSpec((size, length), lambda h: (h, 0)),
            pl.BlockSpec((1, 1, length), lambda h: (h, 0, 0)),
        ],
        out_shape=[
            jax.ShapeDtypeStruct((heads * size, length), bf16),
            jax.ShapeDtypeStruct((heads, 1, length), f32),
        ],
        scratch_shapes=[
            pltpu.VMEM(((chunks - 1) * LANES, LANES), f32),
            pltpu.VMEM((length, 2 * size), bf16),
            pltpu.VMEM((size + 16, length), bf16),
            pltpu.VMEM((length, BLOCK), f32),
        ],
        compiler_params=pltpu.CompilerParams(vmem_limit_bytes=48 * 1024 * 1024),
        cost_estimate=pl.CostEstimate(
            flops=elements * 64 * 4 * 4, bytes_accessed=8 * 1024 * 1024, transcendentals=elements
        ),
    )(offsets, qkv, qkv, qkv)


def attention_backward(offsets, qkv, grad, mixed, logs, heads):
    columns, length = qkv.shape
    size = columns // (3 * heads)
    chunks = offsets.shape[1]
    elements = heads * length * length
    rows = pl.BlockSpec((size, length), lambda h: (h, 0))
    return pl.pallas_call(
        backward_kernel,
        grid=(heads,),
        in_specs=[
            pl.BlockSpec((1, chunks, LANES), lambda h: (h, 0, 0)),
            rows,
            pl.BlockSpec((size, length), lambda h: (heads + h, 0)),
            pl.BlockSpec((size, length), lambda h: (2 * heads + h, 0)),
            rows,
            rows,
            pl.BlockSpec((1, 1, length), lambda h: (h, 0, 0)),
        ],
        out_specs=[rows, rows, rows, pl.BlockSpec((1, chunks, LANES), lambda h: (h, 0, 0))],
        out_shape=[jax.ShapeDtypeStruct((heads * size, length), bf16)] * 3
        + [jax.ShapeDtypeStruct((heads, chunks, LANES), f32)],
        scratch_shapes=[
            pltpu.VMEM(((chunks - 1) * LANES, LANES), f32),
            pltpu.VMEM(((chunks - 1) * LANES, LANES), f32),
            pltpu.VMEM((2 * size, length), bf16),
            pltpu.VMEM((length, size), bf16),
            pltpu.VMEM((length, size), bf16),
            pltpu.VMEM((length, 2 * size), bf16),
            pltpu.VMEM((length, size), bf16),
            pltpu.VMEM((1, length), f32),
            pltpu.VMEM((BLOCK, length), bf16),
            pltpu.VMEM((BLOCK, length), bf16),
            pltpu.VMEM((size, length), f32),
        ],
        compiler_params=pltpu.CompilerParams(vmem_limit_bytes=48 * 1024 * 1024),
        cost_estimate=pl.CostEstimate(
            flops=elements * 64 * 10 * 4, bytes_accessed=12 * 1024 * 1024, transcendentals=elements
        ),
    )(offsets, qkv, qkv, qkv, grad, mixed, logs)


def gelu_parts(inner):
    root = math.sqrt(2.0 / math.pi)
    bent = jnp.tanh(root * (inner + 0.044715 * (inner * inner * inner)))
    hidden = 0.5 * inner * (1.0 + bent)
    slope = 0.5 * (1.0 + bent) + 0.5 * inner * (1.0 - bent * bent) * (
        root * (1.0 + 3 * 0.044715 * (inner * inner))
    )
    return hidden, slope


def exchange(rows, axis):
    return lax.all_to_all(rows, axis, split_axis=0, concat_axis=0, tiled=True)


def local(
    tokens,
    attn_norm,
    attn_in,
    attn_out,
    rel_bias,
    buckets,
    ffn_norm,
    router,
    routes,
    expert_in,
    expert_out,
    cotangent,
):
    shards = lax.axis_size("wshard")
    here = lax.axis_index("wshard")
    owner = lax.axis_index("expert")
    rows, width = tokens.shape
    length = rows * shards
    bucket_count, head_total = rel_bias.shape
    heads = head_total // shards
    part = width // shards
    experts = router.shape[1]
    capacity = max(2, 2 * rows // experts)

    small = jnp.concatenate([attn_norm, ffn_norm, router.T.reshape(-1)])
    small_rows = -(-small.shape[0] // (16 * width)) * 16
    small = jnp.pad(small, (0, small_rows * width - small.shape[0])).reshape(small_rows, width)
    gathered = lax.all_gather(jnp.concatenate([tokens, small], axis=0), "wshard", axis=0)
    seq_tokens = gathered[:, :rows].reshape(length, width).astype(f32)
    small_all = gathered[:, rows:].reshape(shards, -1)
    gain_a = small_all[:, :part].reshape(width).astype(f32)
    gain_f = small_all[:, part : 2 * part].reshape(width).astype(f32)
    full_router = (
        small_all[:, 2 * part : (2 + experts) * part]
        .reshape(shards, experts, part)
        .transpose(1, 0, 2)
        .reshape(experts, width)
    )

    sorted_in = attn_in.reshape(part, 3, shards, part).transpose(2, 0, 1, 3).reshape(shards, part, 3 * part)
    own_in = exchange(sorted_in, "wshard").reshape(width, 3 * part)

    seq_normed = (seq_tokens * rms_scale(seq_tokens) * gain_a).astype(bf16)
    qkv = lax.dot_general(
        own_in, seq_normed, (((0,), (1,)), ((), ())), preferred_element_type=f32
    ).astype(bf16)

    route_ids = routes[:, 0]
    route_hot = route_ids[:, None] == jnp.arange(experts, dtype=jnp.int32)[None, :]
    hot_counts = route_hot.astype(jnp.int32)
    slot_rank = jnp.sum((jnp.cumsum(hot_counts, axis=0) - 1) * hot_counts, axis=1)
    slot_index = route_ids * capacity + slot_rank
    slots = experts * capacity
    place = (jnp.arange(slots, dtype=jnp.int32)[:, None] == slot_index[None, :]).astype(bf16)

    def dispatch(values):
        placed = jnp.dot(place, values, preferred_element_type=f32).astype(bf16)
        return exchange(placed.reshape(experts, capacity, width), "expert").reshape(slots, width)

    def collect(values):
        returned = exchange(values.reshape(experts, capacity, width), "expert").reshape(slots, width)
        return lax.dot_general(
            place, returned, (((0,), (0,)), ((), ())), preferred_element_type=f32
        )

    weight_in, weight_out = expert_in[0], expert_out[0]
    cot_rows = dispatch(cotangent)
    grad_plain = lax.dot_general(
        cot_rows, weight_out, (((1,), (1,)), ((), ())), preferred_element_type=f32
    )

    chunks = 2 * length // LANES
    offset_ids = jnp.concatenate([jnp.full((1,), -1, jnp.int32), buckets[::-1]])
    offset_table = (offset_ids[:, None] == jnp.arange(bucket_count, dtype=jnp.int32)[None, :]).astype(f32)
    own_bias = lax.dynamic_slice_in_dim(rel_bias, here * heads, heads, 1).astype(f32)
    offsets = jnp.einsum("bh,ob->ho", own_bias, offset_table, precision=highest).reshape(
        heads, chunks, LANES
    )
    mixed_own, logs = attention_forward(offsets, qkv, heads)

    full_out = lax.all_gather(attn_out, "wshard", axis=0, tiled=True)
    full_in = lax.all_gather(
        sorted_in.transpose(1, 0, 2).reshape(part, 3 * width), "wshard", axis=0, tiled=True
    )

    def to_tokens(values):
        pieces = values.reshape(values.shape[0], shards, rows).transpose(1, 0, 2)
        return exchange(pieces, "wshard").reshape(shards * values.shape[0], rows)

    mixed_heads = to_tokens(mixed_own)
    start_rows = tokens.astype(f32)
    branch = lax.dot_general(
        mixed_heads, full_out, (((0,), (0,)), ((), ())), preferred_element_type=f32
    )
    middle = start_rows + branch
    scale_f = rms_scale(middle)
    normed_f = (middle * scale_f * gain_f).astype(bf16)
    arrived = dispatch(normed_f)

    def route_probs(values):
        logits = lax.dot_general(
            values, full_router, (((1,), (1,)), ((), ())), preferred_element_type=f32
        )
        shifted = jnp.exp(logits - jnp.max(logits, axis=-1, keepdims=True))
        return shifted / jnp.sum(shifted, axis=-1, keepdims=True)

    probs = route_probs(arrived)
    own_hot = jnp.arange(experts, dtype=jnp.int32)[None, :] == owner
    gate = jnp.sum(jnp.where(own_hot, probs, 0.0), axis=-1, keepdims=True)
    inner = jnp.dot(arrived, weight_in, preferred_element_type=f32)
    hidden, slope = gelu_parts(inner)
    grad_gate = jnp.sum(hidden * grad_plain, axis=-1, keepdims=True)
    grad_inner = (slope * (gate * grad_plain)).astype(bf16)
    hidden = hidden.astype(bf16)
    grad_logits = (probs * (jnp.where(own_hot, grad_gate, 0.0) - gate * grad_gate)).astype(bf16)
    row_grads = lax.dot_general(
        grad_inner, weight_in, (((1,), (1,)), ((), ())), preferred_element_type=f32
    ) + jnp.dot(grad_logits, full_router, preferred_element_type=f32)
    grad_normed_f = collect(row_grads.astype(bf16))

    results = jnp.dot(hidden, weight_out, preferred_element_type=f32).astype(bf16)
    expert_result = collect(results)
    own_probs = route_probs(normed_f)
    gate_prob = jnp.sum(jnp.where(route_hot, own_probs, 0.0), axis=-1, keepdims=True)
    mixed = (middle + gate_prob * expert_result).astype(bf16)

    grad_result = (gate * cot_rows.astype(f32)).astype(bf16)
    local_out = lax.dot_general(
        hidden, grad_result, (((0,), (0,)), ((), ())), preferred_element_type=f32
    )
    local_in = lax.dot_general(
        arrived, grad_inner, (((0,), (0,)), ((), ())), preferred_element_type=f32
    )
    local_router = lax.dot_general(
        arrived, grad_logits, (((0,), (0,)), ((), ())), preferred_element_type=f32
    )
    grad_expert_in = lax.psum_scatter(
        local_in.astype(bf16), "wshard", scatter_dimension=1, tiled=True
    ).astype(f32)[None]
    grad_expert_out = lax.psum_scatter(
        local_out.astype(bf16), "wshard", scatter_dimension=0, tiled=True
    ).astype(f32)[None]

    grad_out = cotangent.astype(f32)
    grad_middle_norm, grad_gain_f = norm_back(grad_normed_f, middle, scale_f, gain_f)
    grad_middle = grad_out + grad_middle_norm
    grad_branch = grad_middle.astype(bf16)
    grad_mixed = lax.dot_general(
        full_out, grad_branch, (((1,), (1,)), ((), ())), preferred_element_type=f32
    ).astype(bf16)
    grad_own = (
        exchange(grad_mixed.reshape(shards, part, rows), "wshard").transpose(1, 0, 2).reshape(part, length)
    )
    grad_attn_out = jnp.dot(mixed_heads, grad_branch, preferred_element_type=f32)
    grad_query, grad_key, grad_value, grad_offsets = attention_backward(
        offsets, qkv, grad_own, mixed_own, logs, heads
    )
    grad_qkv = jnp.concatenate([grad_query, grad_key, grad_value], axis=0)
    grad_tokens_qkv = to_tokens(grad_qkv)
    grad_normed = lax.dot_general(
        grad_tokens_qkv, full_in, (((0,), (1,)), ((), ())), preferred_element_type=f32
    )
    scale_a = rms_scale(start_rows)
    grad_start, grad_gain_a = norm_back(grad_normed, start_rows, scale_a, gain_a)
    grad_tokens = grad_middle + grad_start

    local_attn_in = lax.dot_general(
        seq_normed, grad_qkv, (((0,), (1,)), ((), ())), preferred_element_type=f32
    )
    summed_in = lax.psum_scatter(local_attn_in, "expert", scatter_dimension=0, tiled=True)
    slim = summed_in.shape[0] // shards
    sum_attn_in = (
        exchange(summed_in.reshape(shards, slim, 3 * part), "wshard")
        .reshape(shards, slim, 3, part)
        .transpose(1, 2, 0, 3)
        .reshape(slim, 3 * width)
    )
    both = ("expert", "wshard")
    sum_attn_out = lax.psum_scatter(grad_attn_out, both, scatter_dimension=0, tiled=True)
    own_offsets = jnp.einsum(
        "ob,ho->bh", offset_table, grad_offsets.reshape(heads, -1), precision=highest
    )
    spread = (jnp.arange(shards) == here).astype(f32)
    local_bias = (own_offsets[:, None, :] * spread[None, :, None]).reshape(bucket_count, head_total)
    grad_rel_bias = lax.psum(local_bias, both)
    sum_gain_a = lax.psum_scatter(grad_gain_a, both, scatter_dimension=0, tiled=True)
    sum_gain_f = lax.psum_scatter(grad_gain_f, both, scatter_dimension=0, tiled=True)
    sum_router = lax.psum_scatter(local_router, both, scatter_dimension=0, tiled=True)
    return (
        mixed,
        grad_tokens,
        sum_gain_a,
        sum_attn_in,
        sum_attn_out,
        grad_rel_bias,
        sum_gain_f,
        sum_router,
        grad_expert_in,
        grad_expert_out,
    )


def solution(mesh):
    placed = (
        P(("expert", "wshard"), None),
        P("wshard"),
        P("wshard", None),
        P("wshard", None),
        P(),
        P(),
        P("wshard"),
        P("wshard", None),
        P(("expert", "wshard"), None),
        P("expert", None, None),
        P("expert", None, None),
        P(("expert", "wshard"), None),
    )
    return jax.shard_map(
        local,
        mesh=mesh,
        in_specs=placed,
        out_specs=(
            P(("expert", "wshard"), None),
            P(("expert", "wshard"), None),
            P(("expert", "wshard")),
            P(("expert", "wshard"), None),
            P(("expert", "wshard"), None),
            P(),
            P(("expert", "wshard")),
            P(("expert", "wshard"), None),
            P("expert", None, "wshard"),
            P("expert", "wshard", None),
        ),
        check_vma=False,
    )
```

```python
import functools
import math

import jax
import jax.numpy as jnp
from jax import lax
from jax.experimental import pallas as pl
from jax.experimental.pallas import tpu as pltpu
from jax.sharding import PartitionSpec as P

epsilon = 1e-06
highest = lax.Precision.HIGHEST
f32 = jnp.float32
bf16 = jnp.bfloat16
LOG2E = math.log2(math.e)
LANES = 128
BLOCK = 256


def rms_scale(values):
    return lax.rsqrt(jnp.mean(values * values, axis=-1, keepdims=True) + epsilon)


def norm_back(grad_normed, values, scale, gain):
    scaled = grad_normed * gain
    inner_mean = jnp.mean(scaled * values, axis=-1, keepdims=True)
    grad_values = scale * scaled - values * (scale * scale * scale) * inner_mean
    return (grad_values, jnp.sum(grad_normed * values * scale, axis=0))


def build_bias(offsets, bias_ref):
    chunks = offsets.shape[0]
    rows = jnp.broadcast_to(offsets[:, None, :], (chunks, 8, LANES)).reshape(chunks * 8, LANES)
    sub = lax.broadcasted_iota(jnp.int32, (chunks * 8, LANES), 0) % 8
    for bit in (1, 2, 4):
        rows = jnp.where((sub & bit) != 0, pltpu.roll(rows, bit, 1), rows)
    lane = lax.broadcasted_iota(jnp.int32, (8, LANES), 1)
    sub8 = lax.broadcasted_iota(jnp.int32, (8, LANES), 0)
    for part in range(LANES // 8):
        turned = pltpu.roll(rows, 8 * part, 1) if part else rows
        upper = lane >= sub8 + 8 * part
        for tile in range(chunks - 1):
            chunk = chunks - 1 - tile
            bias_ref[tile * LANES + 8 * part : tile * LANES + 8 * part + 8, :] = jnp.where(
                upper, turned[chunk * 8 : chunk * 8 + 8], turned[chunk * 8 - 8 : chunk * 8]
            )


def fold_bias(grad_ref, work_ref, chunks):
    lane = lax.broadcasted_iota(jnp.int32, (LANES, LANES), 1)
    sub = lax.broadcasted_iota(jnp.int32, (LANES, LANES), 0)
    upper = lane >= sub
    half = LANES // 2
    for chunk in range(chunks):
        total = None
        if chunk >= 1:
            start = (chunks - 1 - chunk) * LANES
            total = jnp.where(upper, grad_ref[start : start + LANES, :], 0.0)
        if chunk <= chunks - 2:
            start = (chunks - 2 - chunk) * LANES
            lower = jnp.where(upper, 0.0, grad_ref[start : start + LANES, :])
            total = lower if total is None else total + lower
        work_ref[0, chunk * half : (chunk + 1) * half, :] = total[:half]
        work_ref[1, chunk * half : (chunk + 1) * half, :] = total[half:]
    total = work_ref[0] + pltpu.roll(work_ref[1], LANES - half, 1)
    while half > 8:
        half //= 2
        total = total.reshape(chunks, 2, half, LANES)
        total = total[:, 0].reshape(chunks * half, LANES) + pltpu.roll(
            total[:, 1].reshape(chunks * half, LANES), LANES - half, 1
        )
    sub8 = lax.broadcasted_iota(jnp.int32, (chunks * 8, LANES), 0) % 8
    for bit in (1, 2, 4):
        total = jnp.where((sub8 & bit) != 0, pltpu.roll(total, LANES - bit, 1), total)
    return jnp.sum(total.reshape(chunks, 8, LANES), axis=1)


def split_scaled(query):
    scaled = query.astype(f32) * (0.125 * LOG2E)
    high = scaled.astype(bf16)
    low = (scaled - high.astype(f32)).astype(bf16)
    return jnp.concatenate([high, low], axis=0)


def strips(bias_ref, tiles, first, start, count):
    parts = []
    for index in range(count):
        row = (tiles - 1 - (first + index)) * LANES + start
        parts.append(bias_ref[pl.ds(pl.multiple_of(row, LANES), BLOCK), :])
    return jnp.concatenate(parts, axis=1)


def forward_kernel(
    offset_ref, query_ref, key_ref, value_ref, mixed_ref, log_ref, bias_ref, key2_ref, value_aug_ref,
    query2_ref, score_ref, weight_ref, top_ref, total_ref
):
    size, length = query_ref.shape
    tiles = length // LANES
    blocks = length // BLOCK
    across = BLOCK // LANES
    build_bias(offset_ref[0] * LOG2E, bias_ref)
    keys = key_ref[...].astype(f32).T.astype(bf16)
    key2_ref[...] = jnp.concatenate([keys, keys], axis=1)
    value_aug_ref[:size, :] = value_ref[...]
    extra = lax.broadcasted_iota(jnp.int32, (16, length), 0)
    value_aug_ref[size:, :] = jnp.where(extra == 0, 1.0, 0.0).astype(bf16)

    top_ref[...] = jnp.full(top_ref.shape, -jnp.inf, f32)
    total_ref[...] = jnp.zeros_like(total_ref)
    query2_ref[...] = split_scaled(query_ref[...])

    def score_chunk(chunk, carry):
        start = pl.multiple_of(chunk * BLOCK, BLOCK)
        rows = pl.ds(start, BLOCK)
        for block in range(blocks):
            columns = slice(block * BLOCK, (block + 1) * BLOCK)
            scores = jnp.dot(key2_ref[rows, :], query2_ref[:, columns], preferred_element_type=f32)
            scores = scores + strips(bias_ref, tiles, block * across, start, across)
            score_ref[rows, columns] = scores
            peak = jnp.max(scores.reshape(BLOCK // 8, 8, BLOCK), axis=0)
            top_ref[:, columns] = jnp.maximum(top_ref[:, columns], peak)
        return carry

    lax.fori_loop(0, blocks, score_chunk, 0)
    top = jnp.max(top_ref[...], axis=0, keepdims=True)
    top_ref[...] = jnp.broadcast_to(top, top_ref.shape)

    def value_chunk(chunk, carry):
        rows = pl.ds(pl.multiple_of(chunk * BLOCK, BLOCK), BLOCK)
        for block in range(blocks):
            columns = slice(block * BLOCK, (block + 1) * BLOCK)
            weight_ref[:, columns] = jnp.exp2(score_ref[rows, columns] - top_ref[:1, columns]).astype(bf16)
        total_ref[...] += jnp.dot(value_aug_ref[:, rows], weight_ref[...], preferred_element_type=f32)
        return carry

    lax.fori_loop(0, blocks, value_chunk, 0)
    row_total = total_ref[size : size + 1, :]
    mixed_ref[...] = (total_ref[:size, :] / row_total).astype(bf16)
    log_ref[0] = top + jnp.log2(row_total)


def backward_kernel(
    offset_ref,
    query_ref,
    key_ref,
    value_ref,
    grad_ref,
    mixed_ref,
    log_ref,
    dqkv_ref,
    doffset_ref,
    bias_ref,
    dbias_ref,
    query2_ref,
    query_rows_ref,
    grad_rows_ref,
    key2_ref,
    value_rows_ref,
    delta_ref,
    weight_ref,
    score_ref,
    dquery_acc_ref,
    fold_ref,
):
    size, length = query_ref.shape
    tiles = length // LANES
    blocks = length // BLOCK
    across = BLOCK // LANES
    build_bias(offset_ref[0] * LOG2E, bias_ref)
    dbias_ref[...] = jnp.zeros_like(dbias_ref)
    query2_ref[...] = split_scaled(query_ref[...])
    query_rows_ref[...] = query_ref[...].astype(f32).T.astype(bf16)
    grad = grad_ref[...].astype(f32)
    grad_rows_ref[...] = grad.T.astype(bf16)
    keys = key_ref[...].astype(f32).T.astype(bf16)
    key2_ref[...] = jnp.concatenate([keys, keys], axis=1)
    value_rows_ref[...] = value_ref[...].astype(f32).T.astype(bf16)
    delta_ref[...] = jnp.sum(grad * mixed_ref[...].astype(f32), axis=0, keepdims=True)
    dquery_acc_ref[...] = jnp.zeros_like(dquery_acc_ref)

    def one_chunk(chunk, carry):
        start = pl.multiple_of(chunk * BLOCK, BLOCK)
        rows = pl.ds(start, BLOCK)
        for block in range(blocks):
            columns = slice(block * BLOCK, (block + 1) * BLOCK)
            scores = jnp.dot(key2_ref[rows, :], query2_ref[:, columns], preferred_element_type=f32)
            scores = scores + strips(bias_ref, tiles, block * across, start, across)
            weights = jnp.exp2(scores - log_ref[0, :, columns])
            weight_ref[:, columns] = weights.astype(bf16)
            dweights = jnp.dot(value_rows_ref[rows, :], grad_ref[:, columns], preferred_element_type=f32)
            dscores = weights * (dweights - delta_ref[:, columns])
            for index in range(across):
                row = (tiles - 1 - (block * across + index)) * LANES + start
                place = pl.ds(pl.multiple_of(row, LANES), BLOCK)
                dbias_ref[place, :] += dscores[:, index * LANES : (index + 1) * LANES]
            score_ref[:, columns] = dscores.astype(bf16)
        dquery_acc_ref[...] += jnp.dot(key_ref[:, rows], score_ref[...], preferred_element_type=f32)
        dvalue = jnp.dot(weight_ref[...], grad_rows_ref[...], preferred_element_type=f32)
        dkey = jnp.dot(score_ref[...], query_rows_ref[...], preferred_element_type=f32) * 0.125
        dqkv_ref[2 * size :, rows] = dvalue.T.astype(bf16)
        dqkv_ref[size : 2 * size, rows] = dkey.T.astype(bf16)
        return carry

    lax.fori_loop(0, blocks, one_chunk, 0)
    dqkv_ref[:size, :] = (dquery_acc_ref[...] * 0.125).astype(bf16)
    doffset_ref[0] = fold_bias(dbias_ref, fold_ref, offset_ref.shape[1])


def attention_forward(offsets, qkv, heads):
    columns, length = qkv.shape
    size = columns // (3 * heads)
    chunks = offsets.shape[1]
    elements = heads * length * length
    return pl.pallas_call(
        forward_kernel,
        grid=(heads,),
        in_specs=[
            pl.BlockSpec((1, chunks, LANES), lambda h: (h, 0, 0)),
            pl.BlockSpec((size, length), lambda h: (h, 0)),
            pl.BlockSpec((size, length), lambda h: (heads + h, 0)),
            pl.BlockSpec((size, length), lambda h: (2 * heads + h, 0)),
        ],
        out_specs=[
            pl.BlockSpec((size, length), lambda h: (h, 0)),
            pl.BlockSpec((1, 1, length), lambda h: (h, 0, 0)),
        ],
        out_shape=[
            jax.ShapeDtypeStruct((heads * size, length), bf16),
            jax.ShapeDtypeStruct((heads, 1, length), f32),
        ],
        scratch_shapes=[
            pltpu.VMEM(((chunks - 1) * LANES, LANES), f32),
            pltpu.VMEM((length, 2 * size), bf16),
            pltpu.VMEM((size + 16, length), bf16),
            pltpu.VMEM((2 * size, length), bf16),
            pltpu.VMEM((length, length), f32),
            pltpu.VMEM((BLOCK, length), bf16),
            pltpu.VMEM((8, length), f32),
            pltpu.VMEM((size + 16, length), f32),
        ],
        compiler_params=pltpu.CompilerParams(vmem_limit_bytes=48 * 1024 * 1024),
        cost_estimate=pl.CostEstimate(
            flops=elements * 64 * 4 * 4, bytes_accessed=8 * 1024 * 1024, transcendentals=elements
        ),
    )(offsets, qkv, qkv, qkv)


def attention_backward(offsets, qkv, grad, mixed, logs, heads, first, count):
    columns, length = qkv.shape
    size = columns // (3 * heads)
    chunks = offsets.shape[1]
    elements = count * length * length
    rows = pl.BlockSpec((size, length), lambda h: (first + h, 0))
    return pl.pallas_call(
        backward_kernel,
        grid=(count,),
        in_specs=[
            pl.BlockSpec((1, chunks, LANES), lambda h: (first + h, 0, 0)),
            rows,
            pl.BlockSpec((size, length), lambda h: (heads + first + h, 0)),
            pl.BlockSpec((size, length), lambda h: (2 * heads + first + h, 0)),
            rows,
            rows,
            pl.BlockSpec((1, 1, length), lambda h: (first + h, 0, 0)),
        ],
        out_specs=[
            pl.BlockSpec((3 * size, length), lambda h: (h, 0)),
            pl.BlockSpec((1, chunks, LANES), lambda h: (h, 0, 0)),
        ],
        out_shape=[
            jax.ShapeDtypeStruct((count * 3 * size, length), bf16),
            jax.ShapeDtypeStruct((count, chunks, LANES), f32),
        ],
        scratch_shapes=[
            pltpu.VMEM(((chunks - 1) * LANES, LANES), f32),
            pltpu.VMEM(((chunks - 1) * LANES, LANES), f32),
            pltpu.VMEM((2 * size, length), bf16),
            pltpu.VMEM((length, size), bf16),
            pltpu.VMEM((length, size), bf16),
            pltpu.VMEM((length, 2 * size), bf16),
            pltpu.VMEM((length, size), bf16),
            pltpu.VMEM((1, length), f32),
            pltpu.VMEM((BLOCK, length), bf16),
            pltpu.VMEM((BLOCK, length), bf16),
            pltpu.VMEM((size, length), f32),
            pltpu.VMEM((2, chunks * LANES // 2, LANES), f32),
        ],
        compiler_params=pltpu.CompilerParams(vmem_limit_bytes=48 * 1024 * 1024),
        cost_estimate=pl.CostEstimate(
            flops=elements * 64 * 10 * 7, bytes_accessed=4 * 1024 * 1024, transcendentals=elements
        ),
    )(offsets, qkv, qkv, qkv, grad, mixed, logs)


def project_kernel(here_ref, gain_ref, *refs):
    shards = (len(refs) - 3) // 2
    tokens, weights = refs[:shards], refs[shards : 2 * shards]
    normed_ref, qkv_ref, weight_ref = refs[2 * shards :]
    here = here_ref[0]
    rows = qkv_ref.shape[1] // shards
    part = weights[0].shape[0]
    for index in range(shards):
        start = pl.multiple_of((here ^ index) * part, part)
        weight_ref[pl.ds(start, part), :] = weights[index][...]
    gain = gain_ref[...]
    for index in range(shards):
        start = pl.multiple_of((here ^ index) * rows, rows)
        values = tokens[index][:rows, :].astype(f32)
        normed = (values * rms_scale(values) * gain).astype(bf16)
        normed_ref[pl.ds(start, rows), :] = normed
        qkv_ref[:, pl.ds(start, rows)] = lax.dot_general(
            weight_ref[...], normed, (((0,), (1,)), ((), ())), preferred_element_type=f32
        ).astype(bf16)


def project(here, gain, tokens, weights, rows):
    shards = len(tokens)
    width, columns = gain.shape[0], weights[0].shape[1]
    whole = pl.BlockSpec(memory_space=pltpu.VMEM)
    return pl.pallas_call(
        project_kernel,
        in_specs=[pl.BlockSpec(memory_space=pltpu.SMEM)] + [whole] * (1 + 2 * shards),
        out_specs=[whole, whole],
        out_shape=[
            jax.ShapeDtypeStruct((shards * rows, width), bf16),
            jax.ShapeDtypeStruct((columns, shards * rows), bf16),
        ],
        scratch_shapes=[pltpu.VMEM((width, columns), bf16)],
        compiler_params=pltpu.CompilerParams(vmem_limit_bytes=48 * 1024 * 1024),
        cost_estimate=pl.CostEstimate(
            flops=2 * shards * rows * width * columns, bytes_accessed=12 * 1024 * 1024, transcendentals=0
        ),
    )(here.reshape(1), gain.reshape(1, width), *tokens, *weights)


def expert_kernel(
    owner_ref,
    arrived_ref,
    router_ref,
    weight_ref,
    plain_ref,
    hidden_ref,
    inner_ref,
    rows_ref,
    logits_ref,
    gate_out_ref,
    probs_ref,
    gate_ref,
    sum_ref,
    total_ref,
):
    step = pl.program_id(0)
    slots = arrived_ref.shape[0]
    experts = router_ref.shape[0]
    chunk = 256
    own = lax.broadcasted_iota(jnp.int32, (1, experts), 1) == owner_ref[0]

    @pl.when(step == 0)
    def start():
        logits = lax.dot_general(
            arrived_ref[...], router_ref[...], (((1,), (1,)), ((), ())), preferred_element_type=f32
        )
        shifted = jnp.exp(logits - jnp.max(logits, axis=-1, keepdims=True))
        probs = shifted / jnp.sum(shifted, axis=-1, keepdims=True)
        probs_ref[...] = probs
        gate = jnp.sum(jnp.where(own, probs, 0.0), axis=-1, keepdims=True)
        gate_ref[...] = jnp.broadcast_to(gate, gate_ref.shape)
        sum_ref[...] = jnp.zeros_like(sum_ref)
        total_ref[...] = jnp.zeros_like(total_ref)

    for first in range(0, slots, chunk):
        rows = slice(first, first + chunk)
        inner = jnp.dot(arrived_ref[rows, :], weight_ref[...], preferred_element_type=f32)
        plain = plain_ref[rows, :]
        hidden, slope = gelu_parts(inner)
        hidden_ref[rows, :] = hidden.astype(bf16)
        product = hidden * plain
        partial = product[:, :LANES]
        for lane in range(LANES, product.shape[1], LANES):
            partial = partial + product[:, lane : lane + LANES]
        sum_ref[rows, :] += partial
        grad = (slope * (gate_ref[rows, :1] * plain)).astype(bf16)
        inner_ref[rows, :] = grad
        total_ref[rows, :] += lax.dot_general(
            grad, weight_ref[...], (((1,), (1,)), ((), ())), preferred_element_type=f32
        )

    @pl.when(step == pl.num_programs(0) - 1)
    def finish():
        gate = gate_ref[:, :1]
        grad_gate = jnp.sum(sum_ref[...], axis=-1, keepdims=True)
        grad_logits = (probs_ref[...] * (jnp.where(own, grad_gate, 0.0) - gate * grad_gate)).astype(bf16)
        logits_ref[...] = grad_logits
        gate_out_ref[...] = gate
        rows_ref[...] = (
            total_ref[...] + jnp.dot(grad_logits, router_ref[...], preferred_element_type=f32)
        ).astype(bf16)


def expert_rows(owner, arrived, router, weight, plain):
    slots, width = arrived.shape
    experts = router.shape[0]
    hidden_width = weight.shape[1]
    block = min(512, hidden_width)
    return pl.pallas_call(
        expert_kernel,
        grid=(hidden_width // block,),
        in_specs=[
            pl.BlockSpec(memory_space=pltpu.SMEM),
            pl.BlockSpec((slots, width), lambda i: (0, 0)),
            pl.BlockSpec((experts, width), lambda i: (0, 0)),
            pl.BlockSpec((width, block), lambda i: (0, i)),
            pl.BlockSpec((slots, block), lambda i: (0, i)),
        ],
        out_specs=[
            pl.BlockSpec((slots, block), lambda i: (0, i)),
            pl.BlockSpec((slots, block), lambda i: (0, i)),
            pl.BlockSpec((slots, width), lambda i: (0, 0)),
            pl.BlockSpec((slots, experts), lambda i: (0, 0)),
            pl.BlockSpec((slots, 1), lambda i: (0, 0)),
        ],
        out_shape=[
            jax.ShapeDtypeStruct((slots, hidden_width), bf16),
            jax.ShapeDtypeStruct((slots, hidden_width), bf16),
            jax.ShapeDtypeStruct((slots, width), bf16),
            jax.ShapeDtypeStruct((slots, experts), bf16),
            jax.ShapeDtypeStruct((slots, 1), f32),
        ],
        scratch_shapes=[
            pltpu.VMEM((slots, experts), f32),
            pltpu.VMEM((slots, LANES), f32),
            pltpu.VMEM((slots, LANES), f32),
            pltpu.VMEM((slots, width), f32),
        ],
        compiler_params=pltpu.CompilerParams(vmem_limit_bytes=48 * 1024 * 1024),
        cost_estimate=pl.CostEstimate(
            flops=4 * slots * width * hidden_width,
            bytes_accessed=32 * 1024 * 1024,
            transcendentals=slots * hidden_width,
        ),
    )(owner.reshape(1), arrived, router, weight, plain)


def gelu_parts(inner):
    root = math.sqrt(2.0 / math.pi)
    bent = jnp.tanh(root * (inner + 0.044715 * (inner * inner * inner)))
    hidden = 0.5 * inner * (1.0 + bent)
    slope = 0.5 * (1.0 + bent) + 0.5 * inner * (1.0 - bent * bent) * (
        root * (1.0 + 3 * 0.044715 * (inner * inner))
    )
    return hidden, slope


def exchange(rows, axis):
    return lax.all_to_all(rows, axis, split_axis=0, concat_axis=0, tiled=True)


def swap(values, step, axis="wshard"):
    return lax.ppermute(values, axis, [(i, i ^ step) for i in range(lax.axis_size(axis))])


def ordered(pieces, here):
    bit = 1
    while bit < len(pieces):
        turned = (here & bit) != 0
        pieces = [jnp.where(turned, pieces[i ^ bit], pieces[i]) for i in range(len(pieces))]
        bit *= 2
    return pieces


def gather_pieces(values, shards):
    pieces = [values]
    step = shards // 2
    far = []
    while step >= 1:
        far.append(step)
        step //= 2
    found = {0: values}
    for step in far:
        for index in list(found):
            found[index ^ step] = swap(found[index], step)
    return [found[index] for index in range(shards)]


def exchange_pieces(piece_for, shards, here):
    return [piece_for(here)] + [swap(piece_for(here ^ step), step) for step in range(1, shards)]


def tie(*values):
    return lax.optimization_barrier(values)


def local(
    tokens,
    attn_norm,
    attn_in,
    attn_out,
    rel_bias,
    buckets,
    ffn_norm,
    router,
    routes,
    expert_in,
    expert_out,
    cotangent,
):
    shards = lax.axis_size("wshard")
    here = lax.axis_index("wshard")
    groups = lax.axis_size("expert")
    owner = lax.axis_index("expert")
    rows, width = tokens.shape
    length = rows * shards
    bucket_count, head_total = rel_bias.shape
    heads = head_total // shards
    part = width // shards
    size = part // heads
    experts = router.shape[1]
    capacity = max(2, 2 * rows // experts)

    small = jnp.concatenate([attn_norm, ffn_norm, router.T.reshape(-1)])
    small_rows = -(-small.shape[0] // (16 * width)) * 16
    small = jnp.pad(small, (0, small_rows * width - small.shape[0])).reshape(small_rows, width)
    gathered = gather_pieces(jnp.concatenate([tokens, small], axis=0), shards)
    small_all = jnp.stack(ordered([piece[rows:] for piece in gathered], here)).reshape(shards, -1)
    gain_a = small_all[:, :part].reshape(width).astype(f32)
    gain_f = small_all[:, part : 2 * part].reshape(width).astype(f32)
    full_router = (
        small_all[:, 2 * part : (2 + experts) * part]
        .reshape(shards, experts, part)
        .transpose(1, 0, 2)
        .reshape(experts, width)
    )

    split_in = attn_in.reshape(part, 3, shards, heads, size)
    sorted_in = split_in.transpose(2, 0, 1, 3, 4).reshape(shards, part, 3 * part)
    own_in = exchange_pieces(
        lambda w: lax.dynamic_index_in_dim(sorted_in, w, 0, keepdims=False), shards, here
    )

    route_ids = routes[:, 0]
    route_hot = route_ids[:, None] == jnp.arange(experts, dtype=jnp.int32)[None, :]
    hot_counts = route_hot.astype(jnp.int32)
    slot_rank = jnp.sum((jnp.cumsum(hot_counts, axis=0) - 1) * hot_counts, axis=1)
    slot_index = route_ids * capacity + slot_rank
    slots = experts * capacity
    place = (jnp.arange(slots, dtype=jnp.int32)[:, None] == slot_index[None, :]).astype(bf16)

    def dispatch(values):
        placed = jnp.dot(place, values, preferred_element_type=f32).astype(bf16)
        return exchange(placed.reshape(experts, capacity, width), "expert").reshape(slots, width)

    def collect(returned):
        return lax.dot_general(
            place, returned, (((0,), (0,)), ((), ())), preferred_element_type=f32
        )

    def send_back(values):
        return exchange(values.reshape(experts, capacity, width), "expert").reshape(slots, width)

    weight_in, weight_out = expert_in[0], expert_out[0]
    cot_rows = dispatch(cotangent)

    chunks = 2 * length // LANES
    offset_ids = jnp.concatenate([jnp.full((1,), -1, jnp.int32), buckets[::-1]])
    offset_table = (offset_ids[:, None] == jnp.arange(bucket_count, dtype=jnp.int32)[None, :]).astype(f32)
    own_bias = lax.dynamic_slice_in_dim(rel_bias, here * heads, heads, 1).astype(f32)
    offsets = jnp.einsum("bh,ob->ho", own_bias, offset_table, precision=highest).reshape(
        heads, chunks, LANES
    )
    gathered[-1], attn_out = tie(gathered[-1], attn_out)
    out_pieces = gather_pieces(attn_out, shards)
    seq_normed, qkv = project(here, gain_a, gathered, own_in, rows)
    by_head = split_in.transpose(0, 3, 2, 1, 4).reshape(part, 3 * width)
    qkv, by_head = tie(qkv, by_head)
    in_pieces = gather_pieces(by_head, shards)
    mixed_own, logs = attention_forward(offsets, qkv, heads)
    mixed_own, cot_rows, *out_pieces = tie(mixed_own, cot_rows, *out_pieces)
    full_out = jnp.concatenate(ordered(out_pieces, here), axis=0)

    def token_columns(values):
        return lambda w: lax.dynamic_slice_in_dim(values, w * rows, rows, values.ndim - 1)

    mixed_heads = jnp.concatenate(
        ordered(exchange_pieces(token_columns(mixed_own), shards, here), here), axis=0
    )
    start_rows = tokens.astype(f32)
    branch = lax.dot_general(
        mixed_heads, full_out, (((0,), (0,)), ((), ())), preferred_element_type=f32
    )
    middle = start_rows + branch
    scale_f = rms_scale(middle)
    normed_f = (middle * scale_f * gain_f).astype(bf16)
    arrived = dispatch(normed_f)

    def route_probs(values):
        logits = lax.dot_general(
            values, full_router, (((1,), (1,)), ((), ())), preferred_element_type=f32
        )
        shifted = jnp.exp(logits - jnp.max(logits, axis=-1, keepdims=True))
        return shifted / jnp.sum(shifted, axis=-1, keepdims=True)

    own_probs = route_probs(normed_f)
    gate_prob = jnp.sum(jnp.where(route_hot, own_probs, 0.0), axis=-1, keepdims=True)
    grad_plain = lax.dot_general(
        cot_rows, weight_out, (((1,), (1,)), ((), ())), preferred_element_type=f32
    )
    full_in = jnp.concatenate(ordered(in_pieces, here), axis=0)
    arrived, gate_prob, grad_plain, full_in = tie(arrived, gate_prob, grad_plain, full_in)

    hidden, grad_inner, row_grads, grad_logits, gate = expert_rows(
        owner, arrived, full_router, weight_in, grad_plain
    )
    row_grads_back = send_back(row_grads)

    def scatter_first(piece):
        got = {
            offset: swap(piece(here ^ (offset + 1)).astype(bf16), 1) for offset in range(0, shards, 2)
        }
        kept = {offset: piece(here ^ offset) + value.astype(f32) for offset, value in got.items()}
        step = 2
        while 2 * step < shards:
            kept = {
                offset: kept[offset] + swap(kept[offset + step].astype(bf16), step).astype(f32)
                for offset in range(0, shards, 2 * step)
            }
            step *= 2
        return kept[0], kept[step].astype(bf16)

    def scatter_last(kept, other):
        return kept.astype(f32) + swap(other, shards // 2).astype(f32)

    grad_result = (gate * cot_rows.astype(f32)).astype(bf16)
    block = hidden.shape[1] // shards

    def out_piece(w):
        return lax.dot_general(
            lax.dynamic_slice_in_dim(hidden, w * block, block, 1),
            grad_result,
            (((0,), (0,)), ((), ())),
            preferred_element_type=f32,
        )

    def in_piece(w):
        return lax.dot_general(
            arrived,
            lax.dynamic_slice_in_dim(grad_inner, w * block, block, 1),
            (((0,), (0,)), ((), ())),
            preferred_element_type=f32,
        )

    local_router = lax.dot_general(
        arrived, grad_logits, (((0,), (0,)), ((), ())), preferred_element_type=f32
    )
    out_kept, out_other = scatter_first(out_piece)
    grad_expert_out = scatter_last(out_kept, out_other)
    in_kept, in_other = scatter_first(in_piece)
    row_grads_back, in_kept, in_other, hidden, local_router = tie(
        row_grads_back, in_kept, in_other, hidden, local_router
    )

    grad_normed_f = collect(row_grads_back)
    grad_out = cotangent.astype(f32)
    grad_middle_norm, grad_gain_f = norm_back(grad_normed_f, middle, scale_f, gain_f)
    grad_middle = grad_out + grad_middle_norm
    grad_branch = grad_middle.astype(bf16)
    grad_mixed = lax.dot_general(
        full_out, grad_branch, (((1,), (1,)), ((), ())), preferred_element_type=f32
    ).astype(bf16)
    grad_mixed, grad_expert_out = tie(grad_mixed, grad_expert_out)
    grad_slabs = grad_mixed.reshape(shards, part, rows)
    grad_own = jnp.concatenate(
        ordered(
            exchange_pieces(
                lambda w: lax.dynamic_index_in_dim(grad_slabs, w, 0, keepdims=False), shards, here
            ),
            here,
        ),
        axis=1,
    )
    local_sums = jnp.concatenate(
        [
            jnp.dot(mixed_heads, grad_branch, preferred_element_type=f32).astype(bf16),
            local_router.astype(bf16),
            grad_gain_f.astype(bf16)[:, None],
        ],
        axis=1,
    )
    slab = width // groups
    slim = slab // shards
    local_sums = local_sums.reshape(groups, shards // 2, 2, slim, -1)
    side = here & 1
    sums_kept = lax.dynamic_index_in_dim(local_sums, side, 2, keepdims=False)
    sums_got = swap(lax.dynamic_index_in_dim(local_sums, 1 - side, 2, keepdims=False), 1)
    results = jnp.dot(hidden, weight_out, preferred_element_type=f32).astype(bf16)
    grad_own, results, in_other = tie(grad_own, results, in_other)
    results_back = send_back(results)
    grad_expert_in = scatter_last(in_kept, in_other)

    pairs = [[i + parity for i in range(0, groups, 2)] for parity in range(2)]

    def first_half(values):
        values = values.reshape((groups // 2, 2) + values.shape[1:])
        side = owner & 1
        sent = lax.dynamic_index_in_dim(values, 1 - side, 1, keepdims=False)
        return lax.dynamic_index_in_dim(values, side, 1, keepdims=False), swap(sent, 1, "expert")

    def second_half(kept, got):
        both = (kept.astype(f32) + got.astype(f32)).astype(bf16)
        return lax.all_to_all(both, "expert", 0, 0, axis_index_groups=pairs, tiled=True)

    def run_heads(first, count, grad_own):
        grad_qkv, grad_offsets = attention_backward(
            offsets, qkv, grad_own, mixed_own, logs, heads, first, count
        )
        grad_offsets = jnp.einsum(
            "ob,ho->hb", offset_table, grad_offsets.reshape(count, -1), precision=highest
        )
        return grad_qkv, grad_offsets

    def attn_in_part(grad_qkv):
        return (
            lax.dot_general(seq_normed, grad_qkv, (((0,), (1,)), ((), ())), preferred_element_type=f32)
            .astype(bf16)
            .reshape(groups, slab, -1)
        )

    def token_share(pieces, first, count):
        grads = jnp.concatenate(
            [
                piece.reshape(count, 1, 3 * size, rows)
                for piece in ordered(list(pieces), here)
            ],
            axis=1,
        ).reshape(count * width, rows)
        return lax.dot_general(
            grads,
            full_in[:, first * width : (first + count) * width],
            (((0,), (1,)), ((), ())),
            preferred_element_type=f32,
        )

    early = heads - 1
    attn_in_early = []
    offset_grads = []
    grad_normed = None
    if early:
        grad_qkv, grad_offsets = run_heads(0, early, grad_own)
        offset_grads.append(grad_offsets)
        grad_own, grad_qkv, results_back, sums_got = tie(
            grad_own, grad_qkv, results_back, sums_got
        )
        pieces = exchange_pieces(token_columns(grad_qkv), shards, here)
        attn_in_early = first_half(attn_in_part(grad_qkv))
    sums_back = exchange((sums_kept.astype(f32) + sums_got.astype(f32)).astype(bf16), "expert")
    grad_qkv, grad_offsets = run_heads(early, 1, grad_own)
    offset_grads.append(grad_offsets)
    if early:
        grad_qkv, grad_expert_in, sums_back, attn_in_early, pieces = tie(
            grad_qkv, grad_expert_in, sums_back, attn_in_early, pieces
        )
        grad_normed = token_share(pieces, 0, early)
    pieces = exchange_pieces(token_columns(grad_qkv), shards, here)
    last = attn_in_part(grad_qkv)
    extra = jnp.concatenate(offset_grads, axis=0).reshape(-1).astype(bf16)
    tail_rows = -(-extra.shape[0] // (16 * 3 * size)) * 16
    extra = jnp.pad(extra, (0, tail_rows * 3 * size - extra.shape[0]))
    extra = jnp.broadcast_to(extra.reshape(1, tail_rows, 3 * size), (groups, tail_rows, 3 * size))
    last = first_half(jnp.concatenate([last, extra], axis=1))
    if early:
        space = jnp.zeros((groups // 2, tail_rows, early * 3 * size), bf16)
        last = [
            jnp.concatenate([jnp.concatenate([one, space], axis=1), two], axis=2)
            for one, two in zip(attn_in_early, last)
        ]
    attn_in_sum = jnp.sum(second_half(*last).astype(f32), axis=0)
    share = token_share(pieces, early, 1)
    grad_normed = share if grad_normed is None else grad_normed + share

    expert_result = collect(results_back)
    mixed = (middle + gate_prob * expert_result).astype(bf16)

    some = jnp.sum(sums_back.astype(f32), axis=0)
    total = lax.dynamic_index_in_dim(some, here // 2, 0, keepdims=False)
    for step in range(1, shards // 2):
        total = total + swap(
            lax.dynamic_index_in_dim(some, (here // 2) ^ step, 0, keepdims=False), 2 * step
        )
    some = total
    sum_attn_out, sum_router, sum_gain_f = (
        some[:, :width],
        some[:, width : width + experts],
        some[:, width + experts],
    )

    scale_a = rms_scale(start_rows)
    grad_start, unused = norm_back(grad_normed, start_rows, scale_a, gain_a)
    grad_tokens = grad_middle + grad_start

    own_offsets = attn_in_sum[slab:, early * 3 * size :].reshape(-1)[: heads * bucket_count]
    wide = attn_in_sum[:slab]
    tail_rows = -(-own_offsets.shape[0] // (8 * 3 * part)) * 8
    tail = jnp.pad(own_offsets, (0, tail_rows * 3 * part - own_offsets.shape[0])).reshape(
        tail_rows, 3 * part
    )
    wide = wide.reshape(shards, slim, 3 * part)
    final = ordered(
        exchange_pieces(
            lambda w: jnp.concatenate([lax.dynamic_index_in_dim(wide, w, 0, keepdims=False), tail], axis=0),
            shards,
            here,
        ),
        here,
    )
    sum_attn_in = (
        jnp.stack([piece[:slim] for piece in final], axis=1)
        .reshape(slim, shards, heads, 3, size)
        .transpose(0, 3, 1, 2, 4)
        .reshape(slim, 3 * width)
    )
    grad_rel_bias = jnp.concatenate(
        [
            piece[slim:].reshape(-1)[: heads * bucket_count].reshape(heads, bucket_count)
            for piece in final
        ],
        axis=0,
    ).T
    first = (owner * shards + here) * slim
    own_rows = (
        lax.dynamic_slice_in_dim(full_in, first, slim, 0)
        .reshape(slim, heads, shards, 3, size)
        .transpose(0, 3, 2, 1, 4)
        .reshape(slim, 3 * width)
    )
    sum_gain_a = jnp.sum(own_rows.astype(f32) * sum_attn_in, axis=1) / lax.dynamic_slice_in_dim(
        gain_a, first, slim, 0
    )
    return (
        mixed,
        grad_tokens,
        sum_gain_a,
        sum_attn_in,
        sum_attn_out,
        grad_rel_bias,
        sum_gain_f,
        sum_router,
        grad_expert_in[None],
        grad_expert_out[None],
    )


def solution(mesh):
    placed = (
        P(("expert", "wshard"), None),
        P("wshard"),
        P("wshard", None),
        P("wshard", None),
        P(),
        P(),
        P("wshard"),
        P("wshard", None),
        P(("expert", "wshard"), None),
        P("expert", None, None),
        P("expert", None, None),
        P(("expert", "wshard"), None),
    )
    return jax.shard_map(
        local,
        mesh=mesh,
        in_specs=placed,
        out_specs=(
            P(("expert", "wshard"), None),
            P(("expert", "wshard"), None),
            P(("expert", "wshard")),
            P(("expert", "wshard"), None),
            P(("expert", "wshard"), None),
            P(),
            P(("expert", "wshard")),
            P(("expert", "wshard"), None),
            P("expert", None, "wshard"),
            P("expert", "wshard", None),
        ),
        check_vma=False,
    )
```

```python
import functools
import math

import jax
import jax.numpy as jnp
from jax import lax
from jax.experimental import pallas as pl
from jax.experimental.pallas import tpu as pltpu
from jax.sharding import PartitionSpec as P

epsilon = 1e-06
highest = lax.Precision.HIGHEST
f32 = jnp.float32
bf16 = jnp.bfloat16
LOG2E = math.log2(math.e)
LANES = 128
BLOCK = 256


def rms_scale(values):
    return lax.rsqrt(jnp.mean(values * values, axis=-1, keepdims=True) + epsilon)


def norm_back(grad_normed, values, scale, gain):
    scaled = grad_normed * gain
    inner_mean = jnp.mean(scaled * values, axis=-1, keepdims=True)
    grad_values = scale * scaled - values * (scale * scale * scale) * inner_mean
    return (grad_values, jnp.sum(grad_normed * values * scale, axis=0))


def build_bias(offsets, bias_ref):
    chunks = offsets.shape[0]
    rows = jnp.broadcast_to(offsets[:, None, :], (chunks, 8, LANES)).reshape(chunks * 8, LANES)
    sub = lax.broadcasted_iota(jnp.int32, (chunks * 8, LANES), 0) % 8
    for bit in (1, 2, 4):
        rows = jnp.where((sub & bit) != 0, pltpu.roll(rows, bit, 1), rows)
    lane = lax.broadcasted_iota(jnp.int32, (8, LANES), 1)
    sub8 = lax.broadcasted_iota(jnp.int32, (8, LANES), 0)
    for part in range(LANES // 8):
        turned = pltpu.roll(rows, 8 * part, 1) if part else rows
        upper = lane >= sub8 + 8 * part
        for tile in range(chunks - 1):
            chunk = chunks - 1 - tile
            bias_ref[tile * LANES + 8 * part : tile * LANES + 8 * part + 8, :] = jnp.where(
                upper, turned[chunk * 8 : chunk * 8 + 8], turned[chunk * 8 - 8 : chunk * 8]
            )


def fold_bias(grad_ref, work_ref, chunks):
    lane = lax.broadcasted_iota(jnp.int32, (LANES, LANES), 1)
    sub = lax.broadcasted_iota(jnp.int32, (LANES, LANES), 0)
    upper = lane >= sub
    half = LANES // 2
    for chunk in range(chunks):
        total = None
        if chunk >= 1:
            start = (chunks - 1 - chunk) * LANES
            total = jnp.where(upper, grad_ref[start : start + LANES, :], 0.0)
        if chunk <= chunks - 2:
            start = (chunks - 2 - chunk) * LANES
            lower = jnp.where(upper, 0.0, grad_ref[start : start + LANES, :])
            total = lower if total is None else total + lower
        work_ref[0, chunk * half : (chunk + 1) * half, :] = total[:half]
        work_ref[1, chunk * half : (chunk + 1) * half, :] = total[half:]
    total = work_ref[0] + pltpu.roll(work_ref[1], LANES - half, 1)
    while half > 8:
        half //= 2
        total = total.reshape(chunks, 2, half, LANES)
        total = total[:, 0].reshape(chunks * half, LANES) + pltpu.roll(
            total[:, 1].reshape(chunks * half, LANES), LANES - half, 1
        )
    sub8 = lax.broadcasted_iota(jnp.int32, (chunks * 8, LANES), 0) % 8
    for bit in (1, 2, 4):
        total = jnp.where((sub8 & bit) != 0, pltpu.roll(total, LANES - bit, 1), total)
    return jnp.sum(total.reshape(chunks, 8, LANES), axis=1)


def split_scaled(query):
    scaled = query.astype(f32) * (0.125 * LOG2E)
    high = scaled.astype(bf16)
    low = (scaled - high.astype(f32)).astype(bf16)
    return jnp.concatenate([high, low], axis=0)


def strips(bias_ref, tiles, first, start, count):
    parts = []
    for index in range(count):
        row = (tiles - 1 - (first + index)) * LANES + start
        parts.append(bias_ref[pl.ds(pl.multiple_of(row, LANES), BLOCK), :])
    return jnp.concatenate(parts, axis=1)


def forward_kernel(
    offset_ref, query_ref, key_ref, value_ref, mixed_ref, log_ref, bias_ref, key2_ref, value_aug_ref,
    query2_ref, score_ref, weight_ref, top_ref, total_ref
):
    size, length = query_ref.shape
    tiles = length // LANES
    blocks = length // BLOCK
    across = BLOCK // LANES
    build_bias(offset_ref[0] * LOG2E, bias_ref)
    keys = key_ref[...].astype(f32).T.astype(bf16)
    key2_ref[...] = jnp.concatenate([keys, keys], axis=1)
    value_aug_ref[:size, :] = value_ref[...]
    extra = lax.broadcasted_iota(jnp.int32, (16, length), 0)
    value_aug_ref[size:, :] = jnp.where(extra == 0, 1.0, 0.0).astype(bf16)

    top_ref[...] = jnp.full(top_ref.shape, -jnp.inf, f32)
    total_ref[...] = jnp.zeros_like(total_ref)
    query2_ref[...] = split_scaled(query_ref[...])

    def score_chunk(chunk, carry):
        start = pl.multiple_of(chunk * BLOCK, BLOCK)
        rows = pl.ds(start, BLOCK)
        for block in range(blocks):
            columns = slice(block * BLOCK, (block + 1) * BLOCK)
            scores = jnp.dot(key2_ref[rows, :], query2_ref[:, columns], preferred_element_type=f32)
            scores = scores + strips(bias_ref, tiles, block * across, start, across)
            score_ref[rows, columns] = scores
            peak = jnp.max(scores.reshape(BLOCK // 8, 8, BLOCK), axis=0)
            top_ref[:, columns] = jnp.maximum(top_ref[:, columns], peak)
        return carry

    lax.fori_loop(0, blocks, score_chunk, 0)
    top = jnp.max(top_ref[...], axis=0, keepdims=True)
    top_ref[...] = jnp.broadcast_to(top, top_ref.shape)

    def value_chunk(chunk, carry):
        rows = pl.ds(pl.multiple_of(chunk * BLOCK, BLOCK), BLOCK)
        for block in range(blocks):
            columns = slice(block * BLOCK, (block + 1) * BLOCK)
            weight_ref[:, columns] = jnp.exp2(score_ref[rows, columns] - top_ref[:1, columns]).astype(bf16)
        total_ref[...] += jnp.dot(value_aug_ref[:, rows], weight_ref[...], preferred_element_type=f32)
        return carry

    lax.fori_loop(0, blocks, value_chunk, 0)
    row_total = total_ref[size : size + 1, :]
    mixed_ref[...] = (total_ref[:size, :] / row_total).astype(bf16)
    log_ref[0] = top + jnp.log2(row_total)


def backward_kernel(
    offset_ref,
    query_ref,
    key_ref,
    value_ref,
    grad_ref,
    mixed_ref,
    log_ref,
    dqkv_ref,
    doffset_ref,
    bias_ref,
    dbias_ref,
    query2_ref,
    query_rows_ref,
    grad_rows_ref,
    key2_ref,
    value_rows_ref,
    delta_ref,
    weight_ref,
    score_ref,
    dquery_acc_ref,
    fold_ref,
):
    size, length = query_ref.shape
    tiles = length // LANES
    blocks = length // BLOCK
    across = BLOCK // LANES
    build_bias(offset_ref[0] * LOG2E, bias_ref)
    dbias_ref[...] = jnp.zeros_like(dbias_ref)
    query2_ref[...] = split_scaled(query_ref[...])
    query_rows_ref[...] = query_ref[...].astype(f32).T.astype(bf16)
    grad = grad_ref[...].astype(f32)
    grad_rows_ref[...] = grad.T.astype(bf16)
    keys = key_ref[...].astype(f32).T.astype(bf16)
    key2_ref[...] = jnp.concatenate([keys, keys], axis=1)
    value_rows_ref[...] = value_ref[...].astype(f32).T.astype(bf16)
    delta_ref[...] = jnp.sum(grad * mixed_ref[...].astype(f32), axis=0, keepdims=True)
    dquery_acc_ref[...] = jnp.zeros_like(dquery_acc_ref)

    def one_chunk(chunk, carry):
        start = pl.multiple_of(chunk * BLOCK, BLOCK)
        rows = pl.ds(start, BLOCK)
        for block in range(blocks):
            columns = slice(block * BLOCK, (block + 1) * BLOCK)
            scores = jnp.dot(key2_ref[rows, :], query2_ref[:, columns], preferred_element_type=f32)
            scores = scores + strips(bias_ref, tiles, block * across, start, across)
            weights = jnp.exp2(scores - log_ref[0, :, columns])
            weight_ref[:, columns] = weights.astype(bf16)
            dweights = jnp.dot(value_rows_ref[rows, :], grad_ref[:, columns], preferred_element_type=f32)
            dscores = weights * (dweights - delta_ref[:, columns])
            for index in range(across):
                row = (tiles - 1 - (block * across + index)) * LANES + start
                place = pl.ds(pl.multiple_of(row, LANES), BLOCK)
                dbias_ref[place, :] += dscores[:, index * LANES : (index + 1) * LANES]
            score_ref[:, columns] = dscores.astype(bf16)
        dquery_acc_ref[...] += jnp.dot(key_ref[:, rows], score_ref[...], preferred_element_type=f32)
        dvalue = jnp.dot(weight_ref[...], grad_rows_ref[...], preferred_element_type=f32)
        dkey = jnp.dot(score_ref[...], query_rows_ref[...], preferred_element_type=f32) * 0.125
        dqkv_ref[2 * size :, rows] = dvalue.T.astype(bf16)
        dqkv_ref[size : 2 * size, rows] = dkey.T.astype(bf16)
        return carry

    lax.fori_loop(0, blocks, one_chunk, 0)
    dqkv_ref[:size, :] = (dquery_acc_ref[...] * 0.125).astype(bf16)
    doffset_ref[0] = fold_bias(dbias_ref, fold_ref, offset_ref.shape[1])


def attention_forward(offsets, qkv, heads):
    columns, length = qkv.shape
    size = columns // (3 * heads)
    chunks = offsets.shape[1]
    elements = heads * length * length
    return pl.pallas_call(
        forward_kernel,
        grid=(heads,),
        in_specs=[
            pl.BlockSpec((1, chunks, LANES), lambda h: (h, 0, 0)),
            pl.BlockSpec((size, length), lambda h: (h, 0)),
            pl.BlockSpec((size, length), lambda h: (heads + h, 0)),
            pl.BlockSpec((size, length), lambda h: (2 * heads + h, 0)),
        ],
        out_specs=[
            pl.BlockSpec((size, length), lambda h: (h, 0)),
            pl.BlockSpec((1, 1, length), lambda h: (h, 0, 0)),
        ],
        out_shape=[
            jax.ShapeDtypeStruct((heads * size, length), bf16),
            jax.ShapeDtypeStruct((heads, 1, length), f32),
        ],
        scratch_shapes=[
            pltpu.VMEM(((chunks - 1) * LANES, LANES), f32),
            pltpu.VMEM((length, 2 * size), bf16),
            pltpu.VMEM((size + 16, length), bf16),
            pltpu.VMEM((2 * size, length), bf16),
            pltpu.VMEM((length, length), f32),
            pltpu.VMEM((BLOCK, length), bf16),
            pltpu.VMEM((8, length), f32),
            pltpu.VMEM((size + 16, length), f32),
        ],
        compiler_params=pltpu.CompilerParams(vmem_limit_bytes=48 * 1024 * 1024),
        cost_estimate=pl.CostEstimate(
            flops=elements * 64 * 4 * 4, bytes_accessed=8 * 1024 * 1024, transcendentals=elements
        ),
    )(offsets, qkv, qkv, qkv)


def attention_backward(offsets, qkv, grad, mixed, logs, heads, first, count):
    columns, length = qkv.shape
    size = columns // (3 * heads)
    chunks = offsets.shape[1]
    elements = count * length * length
    rows = pl.BlockSpec((size, length), lambda h: (first + h, 0))
    return pl.pallas_call(
        backward_kernel,
        grid=(count,),
        in_specs=[
            pl.BlockSpec((1, chunks, LANES), lambda h: (first + h, 0, 0)),
            rows,
            pl.BlockSpec((size, length), lambda h: (heads + first + h, 0)),
            pl.BlockSpec((size, length), lambda h: (2 * heads + first + h, 0)),
            rows,
            rows,
            pl.BlockSpec((1, 1, length), lambda h: (first + h, 0, 0)),
        ],
        out_specs=[
            pl.BlockSpec((3 * size, length), lambda h: (h, 0)),
            pl.BlockSpec((1, chunks, LANES), lambda h: (h, 0, 0)),
        ],
        out_shape=[
            jax.ShapeDtypeStruct((count * 3 * size, length), bf16),
            jax.ShapeDtypeStruct((count, chunks, LANES), f32),
        ],
        scratch_shapes=[
            pltpu.VMEM(((chunks - 1) * LANES, LANES), f32),
            pltpu.VMEM(((chunks - 1) * LANES, LANES), f32),
            pltpu.VMEM((2 * size, length), bf16),
            pltpu.VMEM((length, size), bf16),
            pltpu.VMEM((length, size), bf16),
            pltpu.VMEM((length, 2 * size), bf16),
            pltpu.VMEM((length, size), bf16),
            pltpu.VMEM((1, length), f32),
            pltpu.VMEM((BLOCK, length), bf16),
            pltpu.VMEM((BLOCK, length), bf16),
            pltpu.VMEM((size, length), f32),
            pltpu.VMEM((2, chunks * LANES // 2, LANES), f32),
        ],
        compiler_params=pltpu.CompilerParams(vmem_limit_bytes=48 * 1024 * 1024),
        cost_estimate=pl.CostEstimate(
            flops=elements * 64 * 10 * 7, bytes_accessed=4 * 1024 * 1024, transcendentals=elements
        ),
    )(offsets, qkv, qkv, qkv, grad, mixed, logs)


def project_kernel(here_ref, gain_ref, *refs):
    shards = (len(refs) - 3) // 2
    tokens, weights = refs[:shards], refs[shards : 2 * shards]
    normed_ref, qkv_ref, weight_ref = refs[2 * shards :]
    here = here_ref[0]
    rows = qkv_ref.shape[1] // shards
    part = weights[0].shape[0]
    for index in range(shards):
        start = pl.multiple_of((here ^ index) * part, part)
        weight_ref[pl.ds(start, part), :] = weights[index][...]
    gain = gain_ref[...]
    for index in range(shards):
        start = pl.multiple_of((here ^ index) * rows, rows)
        values = tokens[index][:rows, :].astype(f32)
        normed = (values * rms_scale(values) * gain).astype(bf16)
        normed_ref[pl.ds(start, rows), :] = normed
        qkv_ref[:, pl.ds(start, rows)] = lax.dot_general(
            weight_ref[...], normed, (((0,), (1,)), ((), ())), preferred_element_type=f32
        ).astype(bf16)


def project(here, gain, tokens, weights, rows):
    shards = len(tokens)
    width, columns = gain.shape[0], weights[0].shape[1]
    whole = pl.BlockSpec(memory_space=pltpu.VMEM)
    return pl.pallas_call(
        project_kernel,
        in_specs=[pl.BlockSpec(memory_space=pltpu.SMEM)] + [whole] * (1 + 2 * shards),
        out_specs=[whole, whole],
        out_shape=[
            jax.ShapeDtypeStruct((shards * rows, width), bf16),
            jax.ShapeDtypeStruct((columns, shards * rows), bf16),
        ],
        scratch_shapes=[pltpu.VMEM((width, columns), bf16)],
        compiler_params=pltpu.CompilerParams(vmem_limit_bytes=48 * 1024 * 1024),
        cost_estimate=pl.CostEstimate(
            flops=2 * shards * rows * width * columns, bytes_accessed=12 * 1024 * 1024, transcendentals=0
        ),
    )(here.reshape(1), gain.reshape(1, width), *tokens, *weights)


def expert_kernel(
    index_ref,
    arrived_ref,
    router_ref,
    weight_ref,
    plain_ref,
    hidden_ref,
    sorted_ref,
    inner_ref,
    rows_ref,
    logits_ref,
    gate_out_ref,
    probs_ref,
    gate_ref,
    sum_ref,
    total_ref,
):
    step = pl.program_id(0)
    slots = arrived_ref.shape[0]
    experts = router_ref.shape[0]
    chunk = 256
    own = lax.broadcasted_iota(jnp.int32, (1, experts), 1) == index_ref[0]

    @pl.when(step == 0)
    def start():
        logits = lax.dot_general(
            arrived_ref[...], router_ref[...], (((1,), (1,)), ((), ())), preferred_element_type=f32
        )
        shifted = jnp.exp(logits - jnp.max(logits, axis=-1, keepdims=True))
        probs = shifted / jnp.sum(shifted, axis=-1, keepdims=True)
        probs_ref[...] = probs
        gate = jnp.sum(jnp.where(own, probs, 0.0), axis=-1, keepdims=True)
        gate_ref[...] = jnp.broadcast_to(gate, gate_ref.shape)
        sum_ref[...] = jnp.zeros_like(sum_ref)
        total_ref[...] = jnp.zeros_like(total_ref)

    for first in range(0, slots, chunk):
        rows = slice(first, first + chunk)
        inner = jnp.dot(arrived_ref[rows, :], weight_ref[...], preferred_element_type=f32)
        plain = plain_ref[rows, :]
        hidden, slope = gelu_parts(inner)
        low = hidden.astype(bf16)
        hidden_ref[rows, :] = low
        sorted_ref[rows, :] = low
        product = hidden * plain
        partial = product[:, :LANES]
        for lane in range(LANES, product.shape[1], LANES):
            partial = partial + product[:, lane : lane + LANES]
        sum_ref[rows, :] += partial
        grad = (slope * (gate_ref[rows, :1] * plain)).astype(bf16)
        inner_ref[rows, :] = grad
        total_ref[rows, :] += lax.dot_general(
            grad, weight_ref[...], (((1,), (1,)), ((), ())), preferred_element_type=f32
        )

    @pl.when(step == pl.num_programs(0) - 1)
    def finish():
        gate = gate_ref[:, :1]
        grad_gate = jnp.sum(sum_ref[...], axis=-1, keepdims=True)
        grad_logits = (probs_ref[...] * (jnp.where(own, grad_gate, 0.0) - gate * grad_gate)).astype(bf16)
        logits_ref[...] = grad_logits
        gate_out_ref[...] = gate
        rows_ref[...] = (
            total_ref[...] + jnp.dot(grad_logits, router_ref[...], preferred_element_type=f32)
        ).astype(bf16)


def expert_rows(owner, here, shards, arrived, router, weight, plain):
    slots, width = arrived.shape
    experts = router.shape[0]
    hidden_width = weight.shape[1]
    block = hidden_width // shards
    half = shards // 2

    def which(i, index):
        return index[1] ^ jnp.where(i < half, 2 * i + 1, 2 * (i - half))

    return pl.pallas_call(
        expert_kernel,
        grid_spec=pltpu.PrefetchScalarGridSpec(
            num_scalar_prefetch=1,
            grid=(shards,),
            in_specs=[
                pl.BlockSpec((slots, width), lambda i, index: (0, 0)),
                pl.BlockSpec((experts, width), lambda i, index: (0, 0)),
                pl.BlockSpec((width, block), lambda i, index: (0, which(i, index))),
                pl.BlockSpec((slots, block), lambda i, index: (0, which(i, index))),
            ],
            out_specs=[
                pl.BlockSpec((slots, block), lambda i, index: (0, which(i, index))),
                pl.BlockSpec((slots, block), lambda i, index: (0, i)),
                pl.BlockSpec((slots, block), lambda i, index: (0, i)),
                pl.BlockSpec((slots, width), lambda i, index: (0, 0)),
                pl.BlockSpec((slots, experts), lambda i, index: (0, 0)),
                pl.BlockSpec((slots, 1), lambda i, index: (0, 0)),
            ],
            scratch_shapes=[
                pltpu.VMEM((slots, experts), f32),
                pltpu.VMEM((slots, LANES), f32),
                pltpu.VMEM((slots, LANES), f32),
                pltpu.VMEM((slots, width), f32),
            ],
        ),
        out_shape=[
            jax.ShapeDtypeStruct((slots, hidden_width), bf16),
            jax.ShapeDtypeStruct((slots, hidden_width), bf16),
            jax.ShapeDtypeStruct((slots, hidden_width), bf16),
            jax.ShapeDtypeStruct((slots, width), bf16),
            jax.ShapeDtypeStruct((slots, experts), bf16),
            jax.ShapeDtypeStruct((slots, 1), f32),
        ],
        compiler_params=pltpu.CompilerParams(vmem_limit_bytes=52 * 1024 * 1024),
        cost_estimate=pl.CostEstimate(
            flops=4 * slots * width * hidden_width,
            bytes_accessed=32 * 1024 * 1024,
            transcendentals=slots * hidden_width,
        ),
    )(jnp.stack([owner, here]).astype(jnp.int32), arrived, router, weight, plain)


def weight_grad_kernel(small_ref, big_ref, sent_ref, kept_ref, turned_ref):
    step = pl.program_id(0)
    half = pl.num_programs(0) // 2

    @pl.when(step == 0)
    def start():
        turned_ref[...] = small_ref[...].astype(f32).T.astype(bf16)

    product = jnp.dot(turned_ref[...], big_ref[...], preferred_element_type=f32).astype(bf16)

    @pl.when(step < half)
    def store_sent():
        sent_ref[...] = product

    @pl.when(step >= half)
    def store_kept():
        kept_ref[...] = product


def weight_grad(small, big, shards):
    slots, width = small.shape
    block = big.shape[1] // shards
    half = shards // 2
    return pl.pallas_call(
        weight_grad_kernel,
        grid=(shards,),
        in_specs=[
            pl.BlockSpec((slots, width), lambda i: (0, 0)),
            pl.BlockSpec((slots, block), lambda i: (0, i)),
        ],
        out_specs=[
            pl.BlockSpec((width, block), lambda i: (0, jnp.minimum(i, half - 1))),
            pl.BlockSpec((width, block), lambda i: (0, jnp.maximum(i - half, 0))),
        ],
        out_shape=[jax.ShapeDtypeStruct((width, half * block), bf16)] * 2,
        scratch_shapes=[pltpu.VMEM((width, slots), bf16)],
        compiler_params=pltpu.CompilerParams(vmem_limit_bytes=48 * 1024 * 1024),
        cost_estimate=pl.CostEstimate(
            flops=slots * width, bytes_accessed=1024 * 1024, transcendentals=0
        ),
    )(small, big)


def gelu_parts(inner):
    root = math.sqrt(2.0 / math.pi)
    square = inner * inner
    share = 0.5 + 0.5 * jnp.tanh(inner * (root + (root * 0.044715) * square))
    hidden = inner * share
    slope = share + hidden * (1.0 - share) * (2.0 * root + (root * 6 * 0.044715) * square)
    return hidden, slope


def exchange(rows, axis):
    return lax.all_to_all(rows, axis, split_axis=0, concat_axis=0, tiled=True)


def swap(values, step, axis="wshard"):
    return lax.ppermute(values, axis, [(i, i ^ step) for i in range(lax.axis_size(axis))])


def ordered(pieces, here):
    bit = 1
    while bit < len(pieces):
        turned = (here & bit) != 0
        pieces = [jnp.where(turned, pieces[i ^ bit], pieces[i]) for i in range(len(pieces))]
        bit *= 2
    return pieces


def gather_rest(values, far, shards):
    found = {0: values, shards // 2: far}
    step = shards // 4
    while step >= 1:
        for index in list(found):
            found[index ^ step] = swap(found[index], step)
        step //= 2
    return [found[index] for index in range(shards)]


def exchange_pieces(piece_for, shards, here):
    return [piece_for(here)] + [swap(piece_for(here ^ step), step) for step in range(1, shards)]


def tie(*values):
    return lax.optimization_barrier(values)


def local(
    tokens,
    attn_norm,
    attn_in,
    attn_out,
    rel_bias,
    buckets,
    ffn_norm,
    router,
    routes,
    expert_in,
    expert_out,
    cotangent,
):
    shards = lax.axis_size("wshard")
    here = lax.axis_index("wshard")
    groups = lax.axis_size("expert")
    owner = lax.axis_index("expert")
    rows, width = tokens.shape
    length = rows * shards
    bucket_count, head_total = rel_bias.shape
    heads = head_total // shards
    part = width // shards
    size = part // heads
    experts = router.shape[1]
    capacity = max(2, 2 * rows // experts)

    small = jnp.concatenate([attn_norm, ffn_norm, router.T.reshape(-1)])
    small_rows = -(-small.shape[0] // (16 * width)) * 16
    small = jnp.pad(small, (0, small_rows * width - small.shape[0])).reshape(small_rows, width)
    with_small = jnp.concatenate([tokens, small], axis=0)
    far = swap(with_small, shards // 2)
    route_ids = routes[:, 0]
    route_hot = route_ids[:, None] == jnp.arange(experts, dtype=jnp.int32)[None, :]
    hot_counts = route_hot.astype(jnp.int32)
    slot_rank = jnp.sum((jnp.cumsum(hot_counts, axis=0) - 1) * hot_counts, axis=1)
    slot_index = route_ids * capacity + slot_rank
    slots = experts * capacity
    place = (jnp.arange(slots, dtype=jnp.int32)[:, None] == slot_index[None, :]).astype(bf16)

    def put_in_slots(values):
        placed = jnp.dot(place, values, preferred_element_type=f32).astype(bf16)
        return placed.reshape(experts, capacity, width)

    def dispatch(placed):
        return exchange(placed, "expert").reshape(slots, width)

    def collect(returned):
        return lax.dot_general(
            place, returned, (((0,), (0,)), ((), ())), preferred_element_type=f32
        )

    def send_back(values):
        return exchange(values.reshape(experts, capacity, width), "expert").reshape(slots, width)

    weight_in, weight_out = expert_in[0], expert_out[0]
    cot_slots = put_in_slots(cotangent)

    split_in = attn_in.reshape(part, 3, shards, heads, size)
    sorted_in = split_in.transpose(2, 0, 1, 3, 4).reshape(shards, part, 3 * part)
    sent_in = [
        lax.dynamic_index_in_dim(sorted_in, here ^ step, 0, keepdims=False) for step in range(shards)
    ]
    by_head = split_in.transpose(0, 3, 2, 1, 4).reshape(part, 3 * width)
    far, cot_slots, by_head, *unused = tie(far, cot_slots, by_head, *sent_in)
    gathered = gather_rest(with_small, far, shards)
    own_in = [sent_in[0]] + [swap(sent_in[step], step) for step in range(1, shards)]
    small_all = jnp.stack(ordered([piece[rows:] for piece in gathered], here)).reshape(shards, -1)
    gain_a = small_all[:, :part].reshape(width).astype(f32)
    gain_f = small_all[:, part : 2 * part].reshape(width).astype(f32)
    full_router = (
        small_all[:, 2 * part : (2 + experts) * part]
        .reshape(shards, experts, part)
        .transpose(1, 0, 2)
        .reshape(experts, width)
    )

    chunks = 2 * length // LANES
    offset_ids = jnp.concatenate([jnp.full((1,), -1, jnp.int32), buckets[::-1]])
    offset_table = (offset_ids[:, None] == jnp.arange(bucket_count, dtype=jnp.int32)[None, :]).astype(f32)
    own_bias = lax.dynamic_slice_in_dim(rel_bias, here * heads, heads, 1).astype(f32)
    offsets = jnp.einsum("bh,ob->ho", own_bias, offset_table, precision=highest).reshape(
        heads, chunks, LANES
    )
    seq_normed, qkv = project(here, gain_a, gathered, own_in, rows)
    qkv, by_head, attn_out, cot_slots = tie(qkv, by_head, attn_out, cot_slots)
    cot_rows = dispatch(cot_slots)
    far_out = swap(attn_out, shards // 2)
    far_in = swap(by_head, shards // 2)
    mixed_own, logs = attention_forward(offsets, qkv, heads)
    mixed_own, cot_rows, far_out, far_in = tie(mixed_own, cot_rows, far_out, far_in)
    out_pieces = gather_rest(attn_out, far_out, shards)
    in_pieces = gather_rest(by_head, far_in, shards)
    full_out = jnp.concatenate(ordered(out_pieces, here), axis=0)

    def token_columns(values):
        return lambda w: lax.dynamic_slice_in_dim(values, w * rows, rows, values.ndim - 1)

    mixed_heads = jnp.concatenate(
        ordered(exchange_pieces(token_columns(mixed_own), shards, here), here), axis=0
    )
    start_rows = tokens.astype(f32)
    branch = lax.dot_general(
        mixed_heads, full_out, (((0,), (0,)), ((), ())), preferred_element_type=f32
    )
    middle = start_rows + branch
    scale_f = rms_scale(middle)
    normed_f = (middle * scale_f * gain_f).astype(bf16)
    arrived = dispatch(put_in_slots(normed_f))

    def route_probs(values):
        logits = lax.dot_general(
            values, full_router, (((1,), (1,)), ((), ())), preferred_element_type=f32
        )
        shifted = jnp.exp(logits - jnp.max(logits, axis=-1, keepdims=True))
        return shifted / jnp.sum(shifted, axis=-1, keepdims=True)

    own_probs = route_probs(normed_f)
    gate_prob = jnp.sum(jnp.where(route_hot, own_probs, 0.0), axis=-1, keepdims=True)
    grad_plain = lax.dot_general(
        cot_rows, weight_out, (((1,), (1,)), ((), ())), preferred_element_type=f32
    )
    full_in = jnp.concatenate(ordered(in_pieces, here), axis=0)
    arrived, gate_prob, grad_plain, full_in = tie(arrived, gate_prob, grad_plain, full_in)

    hidden, hidden_sorted, grad_inner, row_grads, grad_logits, gate = expert_rows(
        owner, here, shards, arrived, full_router, weight_in, grad_plain
    )
    row_grads_back = send_back(row_grads)

    def scatter_first(sent, kept):
        sums = kept.astype(f32) + swap(sent, 1).astype(f32)
        pieces = jnp.split(sums, shards // 2, axis=1)
        step = 2
        while 2 * step < shards:
            pieces = [
                pieces[index] + swap(pieces[index + 1].astype(bf16), step).astype(f32)
                for index in range(0, len(pieces), 2)
            ]
            step *= 2
        return pieces[0], pieces[1].astype(bf16)

    grad_result = (gate * cot_rows.astype(f32)).astype(bf16)
    out_sent, out_kept = weight_grad(grad_result, hidden_sorted, shards)
    in_sent, in_kept = weight_grad(arrived, grad_inner, shards)
    results = jnp.dot(hidden, weight_out, preferred_element_type=f32).astype(bf16)
    local_router = lax.dot_general(
        arrived, grad_logits, (((0,), (0,)), ((), ())), preferred_element_type=f32
    )
    out_kept, out_other = scatter_first(out_sent, out_kept)
    in_kept, in_other = scatter_first(in_sent, in_kept)
    row_grads_back, out_other, in_kept, in_other, results, local_router = tie(
        row_grads_back, out_other, in_kept, in_other, results, local_router
    )
    results_back = send_back(results)

    grad_normed_f = collect(row_grads_back)
    grad_out = cotangent.astype(f32)
    grad_middle_norm, grad_gain_f = norm_back(grad_normed_f, middle, scale_f, gain_f)
    grad_middle = grad_out + grad_middle_norm
    grad_branch = grad_middle.astype(bf16)
    grad_mixed = lax.dot_general(
        full_out, grad_branch, (((1,), (1,)), ((), ())), preferred_element_type=f32
    ).astype(bf16)
    grad_slabs = grad_mixed.reshape(shards, part, rows)
    grad_own = jnp.concatenate(
        ordered(
            exchange_pieces(
                lambda w: lax.dynamic_index_in_dim(grad_slabs, w, 0, keepdims=False), shards, here
            ),
            here,
        ),
        axis=1,
    )
    slab = width // groups
    slim = slab // shards
    local_sums = jnp.dot(mixed_heads, grad_branch, preferred_element_type=f32).astype(bf16)
    local_sums = local_sums.reshape(groups, shards // 2, 2, slim, width)
    extras = jnp.concatenate([local_router, grad_gain_f[:, None]], axis=1).astype(bf16)
    extras = extras.reshape(groups, shards // 2, 2, slim, experts + 1)

    def rider(side):
        main = lax.dynamic_index_in_dim(local_sums, side, 2, keepdims=False).reshape(groups, -1, width)
        rest = lax.dynamic_index_in_dim(extras, side, 2, keepdims=False).reshape(groups, -1)
        rest_rows = -(-rest.shape[1] // (16 * width)) * 16
        rest = jnp.pad(rest, ((0, 0), (0, rest_rows * width - rest.shape[1])))
        return jnp.concatenate([main, rest.reshape(groups, rest_rows, width)], axis=1)

    side = here & 1
    rider_kept = rider(side)
    rider_got = swap(rider(1 - side), 1)
    grad_own, rider_kept, out_other, in_other = tie(grad_own, rider_kept, out_other, in_other)
    out_got = swap(out_other, shards // 2)
    in_got = swap(in_other, shards // 2)

    def run_heads(first, count, grad_own):
        grad_qkv, grad_offsets = attention_backward(
            offsets, qkv, grad_own, mixed_own, logs, heads, first, count
        )
        grad_offsets = jnp.einsum(
            "ob,ho->hb", offset_table, grad_offsets.reshape(count, -1), precision=highest
        )
        return grad_qkv, grad_offsets

    def attn_in_part(grad_qkv):
        return (
            lax.dot_general(seq_normed, grad_qkv, (((0,), (1,)), ((), ())), preferred_element_type=f32)
            .astype(bf16)
            .reshape(groups, slab, -1)
        )

    def token_share(pieces, first, count):
        grads = jnp.concatenate(
            [
                piece.reshape(count, 1, 3 * size, rows)
                for piece in ordered(list(pieces), here)
            ],
            axis=1,
        ).reshape(count * width, rows)
        return lax.dot_general(
            grads,
            full_in[:, first * width : (first + count) * width],
            (((0,), (1,)), ((), ())),
            preferred_element_type=f32,
        )

    early = heads - 1
    offset_grads = []
    grad_normed = None
    if early:
        grad_qkv, grad_offsets = run_heads(0, early, grad_own)
        offset_grads.append(grad_offsets)
        grad_own, grad_qkv, rider_got = tie(grad_own, grad_qkv, rider_got)
    riders = (rider_kept.astype(f32) + rider_got.astype(f32)).astype(bf16)
    if early:
        block = attn_in_part(grad_qkv)
        fold = block.shape[1] * block.shape[2] // width
        riders = jnp.concatenate([block.reshape(groups, fold, width), riders], axis=1)
        pieces = exchange_pieces(token_columns(grad_qkv), shards, here)
    riders_back = exchange(riders, "expert")
    grad_qkv, grad_offsets = run_heads(early, 1, grad_own)
    if early:
        grad_qkv, grad_offsets, results_back, out_got, in_got, *pieces = tie(
            grad_qkv, grad_offsets, results_back, out_got, in_got, *pieces
        )
    offset_grads.append(grad_offsets)
    last = attn_in_part(grad_qkv)
    extra = jnp.concatenate(offset_grads, axis=0).reshape(-1).astype(bf16)
    tail_rows = -(-extra.shape[0] // (16 * 3 * size)) * 16
    extra = jnp.pad(extra, (0, tail_rows * 3 * size - extra.shape[0]))
    extra = jnp.broadcast_to(extra.reshape(1, tail_rows, 3 * size), (groups, tail_rows, 3 * size))
    last = jnp.concatenate([last, extra], axis=1)
    grad_qkv, last, riders_back = tie(grad_qkv, last, riders_back)
    if early:
        results_back, last, *pieces = tie(results_back, last, *pieces)
        grad_normed = token_share(pieces, 0, early)
    pieces = exchange_pieces(token_columns(grad_qkv), shards, here)
    last_sum = jnp.sum(exchange(last, "expert").astype(f32), axis=0)
    share = token_share(pieces, early, 1)
    grad_normed = share if grad_normed is None else grad_normed + share

    expert_result = collect(results_back)
    mixed = (middle + gate_prob * expert_result).astype(bf16)

    some = jnp.sum(riders_back.astype(f32), axis=0)
    if early:
        attn_in_sum = some[:fold].reshape(slab, early * 3 * size)
        some = some[fold:]
    some_rows = (shards // 2) * slim
    some_out = some[:some_rows].reshape(shards // 2, slim, width)
    some_rest = some[some_rows:].reshape(-1)[: some_rows * (experts + 1)].reshape(
        shards // 2, slim, experts + 1
    )

    scale_a = rms_scale(start_rows)
    grad_start, unused = norm_back(grad_normed, start_rows, scale_a, gain_a)
    grad_tokens = grad_middle + grad_start

    own_offsets = last_sum[slab:].reshape(-1)[: heads * bucket_count]
    wide = last_sum[:slab]
    if early:
        wide = jnp.concatenate([attn_in_sum, wide], axis=1)
    tail_rows = -(-own_offsets.shape[0] // (8 * width)) * 8
    tail = jnp.pad(own_offsets, (0, tail_rows * width - own_offsets.shape[0])).reshape(
        tail_rows, width
    )
    wide = wide.reshape(shards, slim, 3 * part)

    def shares_of(w):
        def pick(values):
            return lax.dynamic_index_in_dim(values, w, 0, keepdims=False)

        return jnp.concatenate([pick(some_out), pick(some_rest)], axis=1)

    some = shares_of(here // 2)
    for step in range(1, shards // 2):
        some = some + swap(shares_of((here // 2) ^ step), 2 * step)
    sum_attn_out, sum_router, sum_gain_f = (
        some[:, :width],
        some[:, width : width + experts],
        some[:, width + experts],
    )
    final = ordered(
        exchange_pieces(
            lambda w: jnp.concatenate(
                [
                    jnp.pad(
                        lax.dynamic_index_in_dim(wide, w, 0, keepdims=False),
                        ((0, 0), (0, width - 3 * part)),
                    ),
                    tail,
                ],
                axis=0,
            ),
            shards,
            here,
        ),
        here,
    )
    sum_attn_in = (
        jnp.stack([piece[:slim, : 3 * part] for piece in final], axis=1)
        .reshape(slim, shards, heads, 3, size)
        .transpose(0, 3, 1, 2, 4)
        .reshape(slim, 3 * width)
    )
    grad_rel_bias = jnp.concatenate(
        [
            piece[slim:].reshape(-1)[: heads * bucket_count].reshape(heads, bucket_count)
            for piece in final
        ],
        axis=0,
    ).T
    first = (owner * shards + here) * slim
    own_rows = (
        lax.dynamic_slice_in_dim(full_in, first, slim, 0)
        .reshape(slim, heads, shards, 3, size)
        .transpose(0, 3, 2, 1, 4)
        .reshape(slim, 3 * width)
    )
    sum_gain_a = jnp.sum(own_rows.astype(f32) * sum_attn_in, axis=1) / lax.dynamic_slice_in_dim(
        gain_a, first, slim, 0
    )
    return (
        mixed,
        grad_tokens,
        sum_gain_a,
        sum_attn_in,
        sum_attn_out,
        grad_rel_bias,
        sum_gain_f,
        sum_router,
        (in_kept + in_got.astype(f32))[None],
        (out_kept + out_got.astype(f32)).T[None],
    )


def solution(mesh):
    placed = (
        P(("expert", "wshard"), None),
        P("wshard"),
        P("wshard", None),
        P("wshard", None),
        P(),
        P(),
        P("wshard"),
        P("wshard", None),
        P(("expert", "wshard"), None),
        P("expert", None, None),
        P("expert", None, None),
        P(("expert", "wshard"), None),
    )
    return jax.shard_map(
        local,
        mesh=mesh,
        in_specs=placed,
        out_specs=(
            P(("expert", "wshard"), None),
            P(("expert", "wshard"), None),
            P(("expert", "wshard")),
            P(("expert", "wshard"), None),
            P(("expert", "wshard"), None),
            P(),
            P(("expert", "wshard")),
            P(("expert", "wshard"), None),
            P("expert", None, "wshard"),
            P("expert", "wshard", None),
        ),
        check_vma=False,
    )
```

```python
import functools
import math

import jax
import jax.numpy as jnp
from jax import lax
from jax.experimental import pallas as pl
from jax.experimental.pallas import tpu as pltpu
from jax.sharding import PartitionSpec as P

epsilon = 1e-06
highest = lax.Precision.HIGHEST
f32 = jnp.float32
bf16 = jnp.bfloat16
LOG2E = math.log2(math.e)
LANES = 128
BLOCK = 256


def rms_scale(values):
    return lax.rsqrt(jnp.mean(values * values, axis=-1, keepdims=True) + epsilon)


def norm_back(grad_normed, values, scale, gain):
    scaled = grad_normed * gain
    inner_mean = jnp.mean(scaled * values, axis=-1, keepdims=True)
    grad_values = scale * scaled - values * (scale * scale * scale) * inner_mean
    return (grad_values, jnp.sum(grad_normed * values * scale, axis=0))


def build_bias(offsets, bias_ref):
    chunks = offsets.shape[0]
    rows = jnp.broadcast_to(offsets[:, None, :], (chunks, 8, LANES)).reshape(chunks * 8, LANES)
    sub = lax.broadcasted_iota(jnp.int32, (chunks * 8, LANES), 0) % 8
    for bit in (1, 2, 4):
        rows = jnp.where((sub & bit) != 0, pltpu.roll(rows, bit, 1), rows)
    lane = lax.broadcasted_iota(jnp.int32, (8, LANES), 1)
    sub8 = lax.broadcasted_iota(jnp.int32, (8, LANES), 0)
    for part in range(LANES // 8):
        turned = pltpu.roll(rows, 8 * part, 1) if part else rows
        upper = lane >= sub8 + 8 * part
        for tile in range(chunks - 1):
            chunk = chunks - 1 - tile
            bias_ref[tile * LANES + 8 * part : tile * LANES + 8 * part + 8, :] = jnp.where(
                upper, turned[chunk * 8 : chunk * 8 + 8], turned[chunk * 8 - 8 : chunk * 8]
            )


def fold_bias(grad_ref, work_ref, chunks):
    lane = lax.broadcasted_iota(jnp.int32, (LANES, LANES), 1)
    sub = lax.broadcasted_iota(jnp.int32, (LANES, LANES), 0)
    upper = lane >= sub
    half = LANES // 2
    for chunk in range(chunks):
        total = None
        if chunk >= 1:
            start = (chunks - 1 - chunk) * LANES
            total = jnp.where(upper, grad_ref[start : start + LANES, :], 0.0)
        if chunk <= chunks - 2:
            start = (chunks - 2 - chunk) * LANES
            lower = jnp.where(upper, 0.0, grad_ref[start : start + LANES, :])
            total = lower if total is None else total + lower
        work_ref[0, chunk * half : (chunk + 1) * half, :] = total[:half]
        work_ref[1, chunk * half : (chunk + 1) * half, :] = total[half:]
    total = work_ref[0] + pltpu.roll(work_ref[1], LANES - half, 1)
    while half > 8:
        half //= 2
        total = total.reshape(chunks, 2, half, LANES)
        total = total[:, 0].reshape(chunks * half, LANES) + pltpu.roll(
            total[:, 1].reshape(chunks * half, LANES), LANES - half, 1
        )
    sub8 = lax.broadcasted_iota(jnp.int32, (chunks * 8, LANES), 0) % 8
    for bit in (1, 2, 4):
        total = jnp.where((sub8 & bit) != 0, pltpu.roll(total, LANES - bit, 1), total)
    return jnp.sum(total.reshape(chunks, 8, LANES), axis=1)


def split_scaled(query):
    scaled = query.astype(f32) * (0.125 * LOG2E)
    high = scaled.astype(bf16)
    low = (scaled - high.astype(f32)).astype(bf16)
    return jnp.concatenate([high, low], axis=0)


def strips(bias_ref, tiles, first, start, count):
    parts = []
    for index in range(count):
        row = (tiles - 1 - (first + index)) * LANES + start
        parts.append(bias_ref[pl.ds(pl.multiple_of(row, LANES), BLOCK), :])
    return jnp.concatenate(parts, axis=1)


def forward_kernel(
    offset_ref, query_ref, key_ref, value_ref, mixed_ref, log_ref, bias_ref, key2_ref, value_aug_ref,
    query2_ref, score_ref, weight_ref, top_ref, total_ref
):
    size, length = query_ref.shape
    tiles = length // LANES
    blocks = length // BLOCK
    across = BLOCK // LANES
    build_bias(offset_ref[0] * LOG2E, bias_ref)
    keys = key_ref[...].astype(f32).T.astype(bf16)
    key2_ref[...] = jnp.concatenate([keys, keys], axis=1)
    value_aug_ref[:size, :] = value_ref[...]
    extra = lax.broadcasted_iota(jnp.int32, (16, length), 0)
    value_aug_ref[size:, :] = jnp.where(extra == 0, 1.0, 0.0).astype(bf16)

    top_ref[...] = jnp.full(top_ref.shape, -jnp.inf, f32)
    total_ref[...] = jnp.zeros_like(total_ref)
    query2_ref[...] = split_scaled(query_ref[...])

    def score_chunk(chunk, carry):
        start = pl.multiple_of(chunk * BLOCK, BLOCK)
        rows = pl.ds(start, BLOCK)
        for block in range(blocks):
            columns = slice(block * BLOCK, (block + 1) * BLOCK)
            scores = jnp.dot(key2_ref[rows, :], query2_ref[:, columns], preferred_element_type=f32)
            scores = scores + strips(bias_ref, tiles, block * across, start, across)
            score_ref[rows, columns] = scores
            peak = jnp.max(scores.reshape(BLOCK // 8, 8, BLOCK), axis=0)
            top_ref[:, columns] = jnp.maximum(top_ref[:, columns], peak)
        return carry

    lax.fori_loop(0, blocks, score_chunk, 0)
    top = jnp.max(top_ref[...], axis=0, keepdims=True)
    top_ref[...] = jnp.broadcast_to(top, top_ref.shape)

    def value_chunk(chunk, carry):
        rows = pl.ds(pl.multiple_of(chunk * BLOCK, BLOCK), BLOCK)
        for block in range(blocks):
            columns = slice(block * BLOCK, (block + 1) * BLOCK)
            weight_ref[:, columns] = jnp.exp2(score_ref[rows, columns] - top_ref[:1, columns]).astype(bf16)
        total_ref[...] += jnp.dot(value_aug_ref[:, rows], weight_ref[...], preferred_element_type=f32)
        return carry

    lax.fori_loop(0, blocks, value_chunk, 0)
    row_total = total_ref[size : size + 1, :]
    mixed_ref[...] = (total_ref[:size, :] / row_total).astype(bf16)
    log_ref[0] = top + jnp.log2(row_total)


def backward_kernel(
    offset_ref,
    query_ref,
    key_ref,
    value_ref,
    grad_ref,
    mixed_ref,
    log_ref,
    dqkv_ref,
    doffset_ref,
    bias_ref,
    dbias_ref,
    query2_ref,
    query_rows_ref,
    grad_rows_ref,
    key2_ref,
    value_rows_ref,
    delta_ref,
    weight_ref,
    score_ref,
    dquery_acc_ref,
    fold_ref,
):
    size, length = query_ref.shape
    tiles = length // LANES
    blocks = length // BLOCK
    across = BLOCK // LANES
    build_bias(offset_ref[0] * LOG2E, bias_ref)
    dbias_ref[...] = jnp.zeros_like(dbias_ref)
    query2_ref[...] = split_scaled(query_ref[...])
    query_rows_ref[...] = query_ref[...].astype(f32).T.astype(bf16)
    grad = grad_ref[...].astype(f32)
    grad_rows_ref[...] = grad.T.astype(bf16)
    keys = key_ref[...].astype(f32).T.astype(bf16)
    key2_ref[...] = jnp.concatenate([keys, keys], axis=1)
    value_rows_ref[...] = value_ref[...].astype(f32).T.astype(bf16)
    delta_ref[...] = jnp.sum(grad * mixed_ref[...].astype(f32), axis=0, keepdims=True)
    dquery_acc_ref[...] = jnp.zeros_like(dquery_acc_ref)

    def one_chunk(chunk, carry):
        start = pl.multiple_of(chunk * BLOCK, BLOCK)
        rows = pl.ds(start, BLOCK)
        for block in range(blocks):
            columns = slice(block * BLOCK, (block + 1) * BLOCK)
            scores = jnp.dot(key2_ref[rows, :], query2_ref[:, columns], preferred_element_type=f32)
            scores = scores + strips(bias_ref, tiles, block * across, start, across)
            weights = jnp.exp2(scores - log_ref[0, :, columns])
            weight_ref[:, columns] = weights.astype(bf16)
            dweights = jnp.dot(value_rows_ref[rows, :], grad_ref[:, columns], preferred_element_type=f32)
            dscores = weights * (dweights - delta_ref[:, columns])
            for index in range(across):
                row = (tiles - 1 - (block * across + index)) * LANES + start
                place = pl.ds(pl.multiple_of(row, LANES), BLOCK)
                dbias_ref[place, :] += dscores[:, index * LANES : (index + 1) * LANES]
            score_ref[:, columns] = dscores.astype(bf16)
        dquery_acc_ref[...] += jnp.dot(key_ref[:, rows], score_ref[...], preferred_element_type=f32)
        dvalue = jnp.dot(weight_ref[...], grad_rows_ref[...], preferred_element_type=f32)
        dkey = jnp.dot(score_ref[...], query_rows_ref[...], preferred_element_type=f32) * 0.125
        dqkv_ref[2 * size :, rows] = dvalue.T.astype(bf16)
        dqkv_ref[size : 2 * size, rows] = dkey.T.astype(bf16)
        return carry

    lax.fori_loop(0, blocks, one_chunk, 0)
    dqkv_ref[:size, :] = (dquery_acc_ref[...] * 0.125).astype(bf16)
    doffset_ref[0] = fold_bias(dbias_ref, fold_ref, offset_ref.shape[1])


def attention_forward(offsets, qkv, heads):
    columns, length = qkv.shape
    size = columns // (3 * heads)
    chunks = offsets.shape[1]
    elements = heads * length * length
    return pl.pallas_call(
        forward_kernel,
        grid=(heads,),
        in_specs=[
            pl.BlockSpec((1, chunks, LANES), lambda h: (h, 0, 0)),
            pl.BlockSpec((size, length), lambda h: (h, 0)),
            pl.BlockSpec((size, length), lambda h: (heads + h, 0)),
            pl.BlockSpec((size, length), lambda h: (2 * heads + h, 0)),
        ],
        out_specs=[
            pl.BlockSpec((size, length), lambda h: (h, 0)),
            pl.BlockSpec((1, 1, length), lambda h: (h, 0, 0)),
        ],
        out_shape=[
            jax.ShapeDtypeStruct((heads * size, length), bf16),
            jax.ShapeDtypeStruct((heads, 1, length), f32),
        ],
        scratch_shapes=[
            pltpu.VMEM(((chunks - 1) * LANES, LANES), f32),
            pltpu.VMEM((length, 2 * size), bf16),
            pltpu.VMEM((size + 16, length), bf16),
            pltpu.VMEM((2 * size, length), bf16),
            pltpu.VMEM((length, length), f32),
            pltpu.VMEM((BLOCK, length), bf16),
            pltpu.VMEM((8, length), f32),
            pltpu.VMEM((size + 16, length), f32),
        ],
        compiler_params=pltpu.CompilerParams(vmem_limit_bytes=48 * 1024 * 1024),
        cost_estimate=pl.CostEstimate(
            flops=elements * 64 * 4 * 4, bytes_accessed=8 * 1024 * 1024, transcendentals=elements
        ),
    )(offsets, qkv, qkv, qkv)


def attention_backward(offsets, qkv, grad, mixed, logs, heads, first, count):
    columns, length = qkv.shape
    size = columns // (3 * heads)
    chunks = offsets.shape[1]
    elements = count * length * length
    rows = pl.BlockSpec((size, length), lambda h: (first + h, 0))
    return pl.pallas_call(
        backward_kernel,
        grid=(count,),
        in_specs=[
            pl.BlockSpec((1, chunks, LANES), lambda h: (first + h, 0, 0)),
            rows,
            pl.BlockSpec((size, length), lambda h: (heads + first + h, 0)),
            pl.BlockSpec((size, length), lambda h: (2 * heads + first + h, 0)),
            rows,
            rows,
            pl.BlockSpec((1, 1, length), lambda h: (first + h, 0, 0)),
        ],
        out_specs=[
            pl.BlockSpec((3 * size, length), lambda h: (h, 0)),
            pl.BlockSpec((1, chunks, LANES), lambda h: (h, 0, 0)),
        ],
        out_shape=[
            jax.ShapeDtypeStruct((count * 3 * size, length), bf16),
            jax.ShapeDtypeStruct((count, chunks, LANES), f32),
        ],
        scratch_shapes=[
            pltpu.VMEM(((chunks - 1) * LANES, LANES), f32),
            pltpu.VMEM(((chunks - 1) * LANES, LANES), f32),
            pltpu.VMEM((2 * size, length), bf16),
            pltpu.VMEM((length, size), bf16),
            pltpu.VMEM((length, size), bf16),
            pltpu.VMEM((length, 2 * size), bf16),
            pltpu.VMEM((length, size), bf16),
            pltpu.VMEM((1, length), f32),
            pltpu.VMEM((BLOCK, length), bf16),
            pltpu.VMEM((BLOCK, length), bf16),
            pltpu.VMEM((size, length), f32),
            pltpu.VMEM((2, chunks * LANES // 2, LANES), f32),
        ],
        compiler_params=pltpu.CompilerParams(vmem_limit_bytes=48 * 1024 * 1024),
        cost_estimate=pl.CostEstimate(
            flops=elements * 64 * 10 * 7, bytes_accessed=4 * 1024 * 1024, transcendentals=elements
        ),
    )(offsets, qkv, qkv, qkv, grad, mixed, logs)


def project_kernel(here_ref, gain_ref, *refs):
    shards = (len(refs) - 3) // 2
    tokens, weights = refs[:shards], refs[shards : 2 * shards]
    normed_ref, qkv_ref, weight_ref = refs[2 * shards :]
    here = here_ref[0]
    rows = qkv_ref.shape[1] // shards
    part = weights[0].shape[0]
    for index in range(shards):
        start = pl.multiple_of((here ^ index) * part, part)
        weight_ref[pl.ds(start, part), :] = weights[index][...]
    gain = gain_ref[...]
    for index in range(shards):
        start = pl.multiple_of((here ^ index) * rows, rows)
        values = tokens[index][:rows, :].astype(f32)
        normed = (values * rms_scale(values) * gain).astype(bf16)
        normed_ref[pl.ds(start, rows), :] = normed
        qkv_ref[:, pl.ds(start, rows)] = lax.dot_general(
            weight_ref[...], normed, (((0,), (1,)), ((), ())), preferred_element_type=f32
        ).astype(bf16)


def project(here, gain, tokens, weights, rows):
    shards = len(tokens)
    width, columns = gain.shape[0], weights[0].shape[1]
    whole = pl.BlockSpec(memory_space=pltpu.VMEM)
    return pl.pallas_call(
        project_kernel,
        in_specs=[pl.BlockSpec(memory_space=pltpu.SMEM)] + [whole] * (1 + 2 * shards),
        out_specs=[whole, whole],
        out_shape=[
            jax.ShapeDtypeStruct((shards * rows, width), bf16),
            jax.ShapeDtypeStruct((columns, shards * rows), bf16),
        ],
        scratch_shapes=[pltpu.VMEM((width, columns), bf16)],
        compiler_params=pltpu.CompilerParams(vmem_limit_bytes=48 * 1024 * 1024),
        cost_estimate=pl.CostEstimate(
            flops=2 * shards * rows * width * columns, bytes_accessed=12 * 1024 * 1024, transcendentals=0
        ),
    )(here.reshape(1), gain.reshape(1, width), *tokens, *weights)


def expert_kernel(
    index_ref,
    arrived_ref,
    router_ref,
    weight_ref,
    plain_ref,
    hidden_ref,
    sorted_ref,
    inner_ref,
    rows_ref,
    logits_ref,
    gate_out_ref,
    probs_ref,
    gate_ref,
    sum_ref,
    total_ref,
):
    step = pl.program_id(0)
    slots = arrived_ref.shape[0]
    experts = router_ref.shape[0]
    chunk = 256
    own = lax.broadcasted_iota(jnp.int32, (1, experts), 1) == index_ref[0]

    @pl.when(step == 0)
    def start():
        logits = lax.dot_general(
            arrived_ref[...], router_ref[...], (((1,), (1,)), ((), ())), preferred_element_type=f32
        )
        shifted = jnp.exp(logits - jnp.max(logits, axis=-1, keepdims=True))
        probs = shifted / jnp.sum(shifted, axis=-1, keepdims=True)
        probs_ref[...] = probs
        gate = jnp.sum(jnp.where(own, probs, 0.0), axis=-1, keepdims=True)
        gate_ref[...] = jnp.broadcast_to(gate, gate_ref.shape)
        sum_ref[...] = jnp.zeros_like(sum_ref)
        total_ref[...] = jnp.zeros_like(total_ref)

    for first in range(0, slots, chunk):
        rows = slice(first, first + chunk)
        inner = jnp.dot(arrived_ref[rows, :], weight_ref[...], preferred_element_type=f32)
        plain = plain_ref[rows, :]
        hidden, slope = gelu_parts(inner)
        low = hidden.astype(bf16)
        hidden_ref[rows, :] = low
        sorted_ref[rows, :] = low
        product = hidden * plain
        partial = product[:, :LANES]
        for lane in range(LANES, product.shape[1], LANES):
            partial = partial + product[:, lane : lane + LANES]
        sum_ref[rows, :] += partial
        grad = (slope * (gate_ref[rows, :1] * plain)).astype(bf16)
        inner_ref[rows, :] = grad
        total_ref[rows, :] += lax.dot_general(
            grad, weight_ref[...], (((1,), (1,)), ((), ())), preferred_element_type=f32
        )

    @pl.when(step == pl.num_programs(0) - 1)
    def finish():
        gate = gate_ref[:, :1]
        grad_gate = jnp.sum(sum_ref[...], axis=-1, keepdims=True)
        grad_logits = (probs_ref[...] * (jnp.where(own, grad_gate, 0.0) - gate * grad_gate)).astype(bf16)
        logits_ref[...] = grad_logits
        gate_out_ref[...] = gate
        rows_ref[...] = (
            total_ref[...] + jnp.dot(grad_logits, router_ref[...], preferred_element_type=f32)
        ).astype(bf16)


def expert_rows(owner, here, shards, arrived, router, weight, plain):
    slots, width = arrived.shape
    experts = router.shape[0]
    hidden_width = weight.shape[1]
    block = hidden_width // shards
    half = shards // 2

    def which(i, index):
        return index[1] ^ jnp.where(i < half, 2 * i + 1, 2 * (i - half))

    return pl.pallas_call(
        expert_kernel,
        grid_spec=pltpu.PrefetchScalarGridSpec(
            num_scalar_prefetch=1,
            grid=(shards,),
            in_specs=[
                pl.BlockSpec((slots, width), lambda i, index: (0, 0)),
                pl.BlockSpec((experts, width), lambda i, index: (0, 0)),
                pl.BlockSpec((width, block), lambda i, index: (0, which(i, index))),
                pl.BlockSpec((slots, block), lambda i, index: (0, which(i, index))),
            ],
            out_specs=[
                pl.BlockSpec((slots, block), lambda i, index: (0, which(i, index))),
                pl.BlockSpec((slots, block), lambda i, index: (0, i)),
                pl.BlockSpec((slots, block), lambda i, index: (0, i)),
                pl.BlockSpec((slots, width), lambda i, index: (0, 0)),
                pl.BlockSpec((slots, experts), lambda i, index: (0, 0)),
                pl.BlockSpec((slots, 1), lambda i, index: (0, 0)),
            ],
            scratch_shapes=[
                pltpu.VMEM((slots, experts), f32),
                pltpu.VMEM((slots, LANES), f32),
                pltpu.VMEM((slots, LANES), f32),
                pltpu.VMEM((slots, width), f32),
            ],
        ),
        out_shape=[
            jax.ShapeDtypeStruct((slots, hidden_width), bf16),
            jax.ShapeDtypeStruct((slots, hidden_width), bf16),
            jax.ShapeDtypeStruct((slots, hidden_width), bf16),
            jax.ShapeDtypeStruct((slots, width), bf16),
            jax.ShapeDtypeStruct((slots, experts), bf16),
            jax.ShapeDtypeStruct((slots, 1), f32),
        ],
        compiler_params=pltpu.CompilerParams(vmem_limit_bytes=52 * 1024 * 1024),
        cost_estimate=pl.CostEstimate(
            flops=4 * slots * width * hidden_width,
            bytes_accessed=32 * 1024 * 1024,
            transcendentals=slots * hidden_width,
        ),
    )(jnp.stack([owner, here]).astype(jnp.int32), arrived, router, weight, plain)


def result_kernel(hidden_ref, weight_ref, result_ref, total_ref):
    step = pl.program_id(0)

    @pl.when(step == 0)
    def start():
        total_ref[...] = jnp.zeros_like(total_ref)

    total_ref[...] += jnp.dot(hidden_ref[...], weight_ref[...], preferred_element_type=f32)

    @pl.when(step == pl.num_programs(0) - 1)
    def finish():
        result_ref[...] = total_ref[...].astype(bf16)


def expert_results(hidden, weight, steps):
    slots, depth = hidden.shape
    width = weight.shape[1]
    block = depth // steps
    return pl.pallas_call(
        result_kernel,
        grid=(steps,),
        in_specs=[
            pl.BlockSpec((slots, block), lambda i: (0, i)),
            pl.BlockSpec((block, width), lambda i: (i, 0)),
        ],
        out_specs=pl.BlockSpec((slots, width), lambda i: (0, 0)),
        out_shape=jax.ShapeDtypeStruct((slots, width), bf16),
        scratch_shapes=[pltpu.VMEM((slots, width), f32)],
        compiler_params=pltpu.CompilerParams(vmem_limit_bytes=48 * 1024 * 1024),
        cost_estimate=pl.CostEstimate(
            flops=slots * width, bytes_accessed=1024 * 1024, transcendentals=0
        ),
    )(hidden, weight)


def weight_grad_kernel(small_ref, big_ref, sent_ref, kept_ref, turned_ref):
    step = pl.program_id(0)
    half = pl.num_programs(0) // 2

    @pl.when(step == 0)
    def start():
        turned_ref[...] = small_ref[...].astype(f32).T.astype(bf16)

    product = jnp.dot(turned_ref[...], big_ref[...], preferred_element_type=f32).astype(bf16)

    @pl.when(step < half)
    def store_sent():
        sent_ref[...] = product

    @pl.when(step >= half)
    def store_kept():
        kept_ref[...] = product


def weight_grad(small, big, shards):
    slots, width = small.shape
    block = big.shape[1] // shards
    half = shards // 2
    return pl.pallas_call(
        weight_grad_kernel,
        grid=(shards,),
        in_specs=[
            pl.BlockSpec((slots, width), lambda i: (0, 0)),
            pl.BlockSpec((slots, block), lambda i: (0, i)),
        ],
        out_specs=[
            pl.BlockSpec((width, block), lambda i: (0, jnp.minimum(i, half - 1))),
            pl.BlockSpec((width, block), lambda i: (0, jnp.maximum(i - half, 0))),
        ],
        out_shape=[jax.ShapeDtypeStruct((width, half * block), bf16)] * 2,
        scratch_shapes=[pltpu.VMEM((width, slots), bf16)],
        compiler_params=pltpu.CompilerParams(vmem_limit_bytes=48 * 1024 * 1024),
        cost_estimate=pl.CostEstimate(
            flops=slots * width, bytes_accessed=1024 * 1024, transcendentals=0
        ),
    )(small, big)


def gelu_parts(inner):
    root = math.sqrt(2.0 / math.pi)
    square = inner * inner
    share = 0.5 + 0.5 * jnp.tanh(inner * (root + (root * 0.044715) * square))
    hidden = inner * share
    slope = share + hidden * (1.0 - share) * (2.0 * root + (root * 6 * 0.044715) * square)
    return hidden, slope


def exchange(rows, axis):
    return lax.all_to_all(rows, axis, split_axis=0, concat_axis=0, tiled=True)


def swap(values, step, axis="wshard"):
    return lax.ppermute(values, axis, [(i, i ^ step) for i in range(lax.axis_size(axis))])


def ordered(pieces, here):
    bit = 1
    while bit < len(pieces):
        turned = (here & bit) != 0
        pieces = [jnp.where(turned, pieces[i ^ bit], pieces[i]) for i in range(len(pieces))]
        bit *= 2
    return pieces


def gather_rest(values, far, shards):
    found = {0: values, shards // 2: far}
    step = shards // 4
    while step >= 1:
        for index in list(found):
            found[index ^ step] = swap(found[index], step)
        step //= 2
    return [found[index] for index in range(shards)]


def exchange_pieces(piece_for, shards, here):
    return [piece_for(here)] + [swap(piece_for(here ^ step), step) for step in range(1, shards)]


def tie(*values):
    return lax.optimization_barrier(values)


def local(
    tokens,
    attn_norm,
    attn_in,
    attn_out,
    rel_bias,
    buckets,
    ffn_norm,
    router,
    routes,
    expert_in,
    expert_out,
    cotangent,
):
    shards = lax.axis_size("wshard")
    here = lax.axis_index("wshard")
    groups = lax.axis_size("expert")
    owner = lax.axis_index("expert")
    rows, width = tokens.shape
    length = rows * shards
    bucket_count, head_total = rel_bias.shape
    heads = head_total // shards
    part = width // shards
    size = part // heads
    experts = router.shape[1]
    capacity = max(2, 2 * rows // experts)

    small = jnp.concatenate([attn_norm, ffn_norm, router.T.reshape(-1)])
    small_rows = -(-small.shape[0] // (16 * width)) * 16
    small = jnp.pad(small, (0, small_rows * width - small.shape[0])).reshape(small_rows, width)
    with_small = jnp.concatenate([tokens, small], axis=0)
    far = swap(with_small, shards // 2)
    route_ids = routes[:, 0]
    route_hot = route_ids[:, None] == jnp.arange(experts, dtype=jnp.int32)[None, :]
    hot_counts = route_hot.astype(jnp.int32)
    slot_rank = jnp.sum((jnp.cumsum(hot_counts, axis=0) - 1) * hot_counts, axis=1)
    slot_index = route_ids * capacity + slot_rank
    slots = experts * capacity
    place = (jnp.arange(slots, dtype=jnp.int32)[:, None] == slot_index[None, :]).astype(bf16)

    def put_in_slots(values):
        placed = jnp.dot(place, values, preferred_element_type=f32).astype(bf16)
        return placed.reshape(experts, capacity, width)

    def dispatch(placed):
        return exchange(placed, "expert").reshape(slots, width)

    def collect(returned):
        return lax.dot_general(
            place, returned, (((0,), (0,)), ((), ())), preferred_element_type=f32
        )

    def send_back(values):
        return exchange(values.reshape(experts, capacity, width), "expert").reshape(slots, width)

    weight_in, weight_out = expert_in[0], expert_out[0]
    cot_slots = put_in_slots(cotangent)

    split_in = attn_in.reshape(part, 3, shards, heads, size)
    sorted_in = split_in.transpose(2, 0, 1, 3, 4).reshape(shards, part, 3 * part)
    sent_in = [
        lax.dynamic_index_in_dim(sorted_in, here ^ step, 0, keepdims=False) for step in range(shards)
    ]
    by_head = split_in.transpose(0, 3, 2, 1, 4).reshape(part, 3 * width)
    far, cot_slots, by_head, *unused = tie(far, cot_slots, by_head, *sent_in)
    gathered = gather_rest(with_small, far, shards)
    own_in = [sent_in[0]] + [swap(sent_in[step], step) for step in range(1, shards)]
    small_all = jnp.stack(ordered([piece[rows:] for piece in gathered], here)).reshape(shards, -1)
    gain_a = small_all[:, :part].reshape(width).astype(f32)
    gain_f = small_all[:, part : 2 * part].reshape(width).astype(f32)
    full_router = (
        small_all[:, 2 * part : (2 + experts) * part]
        .reshape(shards, experts, part)
        .transpose(1, 0, 2)
        .reshape(experts, width)
    )

    chunks = 2 * length // LANES
    offset_ids = jnp.concatenate([jnp.full((1,), -1, jnp.int32), buckets[::-1]])
    offset_table = (offset_ids[:, None] == jnp.arange(bucket_count, dtype=jnp.int32)[None, :]).astype(f32)
    own_bias = lax.dynamic_slice_in_dim(rel_bias, here * heads, heads, 1).astype(f32)
    offsets = jnp.einsum("bh,ob->ho", own_bias, offset_table, precision=highest).reshape(
        heads, chunks, LANES
    )
    seq_normed, qkv = project(here, gain_a, gathered, own_in, rows)
    qkv, by_head, attn_out, cot_slots = tie(qkv, by_head, attn_out, cot_slots)
    cot_rows = dispatch(cot_slots)
    far_out = swap(attn_out, shards // 2)
    far_in = swap(by_head, shards // 2)
    mixed_own, logs = attention_forward(offsets, qkv, heads)
    mixed_own, cot_rows, far_out, far_in = tie(mixed_own, cot_rows, far_out, far_in)
    out_pieces = gather_rest(attn_out, far_out, shards)
    in_pieces = gather_rest(by_head, far_in, shards)
    full_out = jnp.concatenate(ordered(out_pieces, here), axis=0)

    def token_columns(values):
        return lambda w: lax.dynamic_slice_in_dim(values, w * rows, rows, values.ndim - 1)

    mixed_heads = jnp.concatenate(
        ordered(exchange_pieces(token_columns(mixed_own), shards, here), here), axis=0
    )
    start_rows = tokens.astype(f32)
    branch = lax.dot_general(
        mixed_heads, full_out, (((0,), (0,)), ((), ())), preferred_element_type=f32
    )
    middle = start_rows + branch
    scale_f = rms_scale(middle)
    normed_f = (middle * scale_f * gain_f).astype(bf16)
    arrived = dispatch(put_in_slots(normed_f))

    def route_probs(values):
        logits = lax.dot_general(
            values, full_router, (((1,), (1,)), ((), ())), preferred_element_type=f32
        )
        shifted = jnp.exp(logits - jnp.max(logits, axis=-1, keepdims=True))
        return shifted / jnp.sum(shifted, axis=-1, keepdims=True)

    own_probs = route_probs(normed_f)
    gate_prob = jnp.sum(jnp.where(route_hot, own_probs, 0.0), axis=-1, keepdims=True)
    grad_plain = lax.dot_general(
        cot_rows, weight_out, (((1,), (1,)), ((), ())), preferred_element_type=f32
    )
    full_in = jnp.concatenate(ordered(in_pieces, here), axis=0)
    arrived, gate_prob, grad_plain, full_in = tie(arrived, gate_prob, grad_plain, full_in)

    hidden, hidden_sorted, grad_inner, row_grads, grad_logits, gate = expert_rows(
        owner, here, shards, arrived, full_router, weight_in, grad_plain
    )
    row_grads_back = send_back(row_grads)

    def scatter_first(sent, kept):
        return scatter_rest(swap(sent, 1), kept)

    def scatter_rest(got, kept):
        sums = kept.astype(f32) + got.astype(f32)
        pieces = jnp.split(sums, shards // 2, axis=1)
        step = 2
        while 2 * step < shards:
            pieces = [
                pieces[index] + swap(pieces[index + 1].astype(bf16), step).astype(f32)
                for index in range(0, len(pieces), 2)
            ]
            step *= 2
        return pieces[0], pieces[1].astype(bf16)

    grad_result = (gate * cot_rows.astype(f32)).astype(bf16)
    out_sent, out_kept = weight_grad(grad_result, hidden_sorted, shards)
    in_sent, in_kept = weight_grad(arrived, grad_inner, shards)
    results = expert_results(hidden, weight_out, shards)
    local_router = lax.dot_general(
        arrived, grad_logits, (((0,), (0,)), ((), ())), preferred_element_type=f32
    )
    row_grads_back, out_sent, out_kept, in_sent, in_kept, results, local_router = tie(
        row_grads_back, out_sent, out_kept, in_sent, in_kept, results, local_router
    )
    results_back = send_back(results)

    grad_normed_f = collect(row_grads_back)
    grad_out = cotangent.astype(f32)
    grad_middle_norm, grad_gain_f = norm_back(grad_normed_f, middle, scale_f, gain_f)
    grad_middle = grad_out + grad_middle_norm
    grad_branch = grad_middle.astype(bf16)
    grad_mixed = lax.dot_general(
        full_out, grad_branch, (((1,), (1,)), ((), ())), preferred_element_type=f32
    ).astype(bf16)
    grad_slabs = grad_mixed.reshape(shards, part, rows)
    grad_own = jnp.concatenate(
        ordered(
            exchange_pieces(
                lambda w: lax.dynamic_index_in_dim(grad_slabs, w, 0, keepdims=False), shards, here
            ),
            here,
        ),
        axis=1,
    )
    slab = width // groups
    slim = slab // shards
    local_sums = jnp.dot(mixed_heads, grad_branch, preferred_element_type=f32).astype(bf16)
    local_sums = local_sums.reshape(groups, shards // 2, 2, slim, width)
    extras = jnp.concatenate([local_router, grad_gain_f[:, None]], axis=1).astype(bf16)
    extras = extras.reshape(groups, shards // 2, 2, slim, experts + 1)

    def rider(side):
        main = lax.dynamic_index_in_dim(local_sums, side, 2, keepdims=False).reshape(groups, -1, width)
        rest = lax.dynamic_index_in_dim(extras, side, 2, keepdims=False).reshape(groups, -1)
        rest_rows = -(-rest.shape[1] // (16 * width)) * 16
        rest = jnp.pad(rest, ((0, 0), (0, rest_rows * width - rest.shape[1])))
        return jnp.concatenate([main, rest.reshape(groups, rest_rows, width)], axis=1)

    side = here & 1
    rider_kept = rider(side)
    rider_got = swap(rider(1 - side), 1)
    out_kept, out_other = scatter_first(out_sent, out_kept)
    grad_own, rider_kept, out_other = tie(grad_own, rider_kept, out_other)
    out_got = swap(out_other, shards // 2)
    in_sent = swap(in_sent, 1)

    def run_heads(first, count, grad_own):
        grad_qkv, grad_offsets = attention_backward(
            offsets, qkv, grad_own, mixed_own, logs, heads, first, count
        )
        grad_offsets = jnp.einsum(
            "ob,ho->hb", offset_table, grad_offsets.reshape(count, -1), precision=highest
        )
        return grad_qkv, grad_offsets

    def attn_in_part(grad_qkv):
        return (
            lax.dot_general(seq_normed, grad_qkv, (((0,), (1,)), ((), ())), preferred_element_type=f32)
            .astype(bf16)
            .reshape(groups, slab, -1)
        )

    def token_share(pieces, first, count):
        grads = jnp.concatenate(
            [
                piece.reshape(count, 1, 3 * size, rows)
                for piece in ordered(list(pieces), here)
            ],
            axis=1,
        ).reshape(count * width, rows)
        return lax.dot_general(
            grads,
            full_in[:, first * width : (first + count) * width],
            (((0,), (1,)), ((), ())),
            preferred_element_type=f32,
        )

    early = heads - 1
    offset_grads = []
    grad_normed = None
    if early:
        grad_qkv, grad_offsets = run_heads(0, early, grad_own)
        offset_grads.append(grad_offsets)
        grad_own, grad_qkv, rider_got, in_sent, out_got = tie(
            grad_own, grad_qkv, rider_got, in_sent, out_got
        )
    in_kept, in_other = scatter_rest(in_sent, in_kept)
    in_got = swap(in_other, shards // 2)
    riders = (rider_kept.astype(f32) + rider_got.astype(f32)).astype(bf16)
    if early:
        block = attn_in_part(grad_qkv)
        fold = block.shape[1] * block.shape[2] // width
        riders = jnp.concatenate([block.reshape(groups, fold, width), riders], axis=1)
        pieces = exchange_pieces(token_columns(grad_qkv), shards, here)
    riders_back = exchange(riders, "expert")
    grad_qkv, grad_offsets = run_heads(early, 1, grad_own)
    if early:
        grad_qkv, grad_offsets, results_back, in_got, *pieces = tie(
            grad_qkv, grad_offsets, results_back, in_got, *pieces
        )
    offset_grads.append(grad_offsets)
    last = attn_in_part(grad_qkv)
    extra = jnp.concatenate(offset_grads, axis=0).reshape(-1).astype(bf16)
    tail_rows = -(-extra.shape[0] // (16 * 3 * size)) * 16
    extra = jnp.pad(extra, (0, tail_rows * 3 * size - extra.shape[0]))
    extra = jnp.broadcast_to(extra.reshape(1, tail_rows, 3 * size), (groups, tail_rows, 3 * size))
    last = jnp.concatenate([last, extra], axis=1)
    grad_qkv, last, riders_back = tie(grad_qkv, last, riders_back)
    if early:
        results_back, last, *pieces = tie(results_back, last, *pieces)
        grad_normed = token_share(pieces, 0, early)
    pieces = exchange_pieces(token_columns(grad_qkv), shards, here)
    last_sum = jnp.sum(exchange(last, "expert").astype(f32), axis=0)
    share = token_share(pieces, early, 1)
    grad_normed = share if grad_normed is None else grad_normed + share

    expert_result = collect(results_back)
    mixed = (middle + gate_prob * expert_result).astype(bf16)

    some = jnp.sum(riders_back.astype(f32), axis=0)
    if early:
        attn_in_sum = some[:fold].reshape(slab, early * 3 * size)
        some = some[fold:]
    some_rows = (shards // 2) * slim
    some_out = some[:some_rows].reshape(shards // 2, slim, width)
    some_rest = some[some_rows:].reshape(-1)[: some_rows * (experts + 1)].reshape(
        shards // 2, slim, experts + 1
    )

    scale_a = rms_scale(start_rows)
    grad_start, unused = norm_back(grad_normed, start_rows, scale_a, gain_a)
    grad_tokens = grad_middle + grad_start

    own_offsets = last_sum[slab:].reshape(-1)[: heads * bucket_count]
    wide = last_sum[:slab]
    if early:
        wide = jnp.concatenate([attn_in_sum, wide], axis=1)
    tail_rows = -(-own_offsets.shape[0] // (8 * width)) * 8
    tail = jnp.pad(own_offsets, (0, tail_rows * width - own_offsets.shape[0])).reshape(
        tail_rows, width
    )
    wide = wide.reshape(shards, slim, 3 * part)

    def shares_of(w):
        def pick(values):
            return lax.dynamic_index_in_dim(values, w, 0, keepdims=False)

        return jnp.concatenate([pick(some_out), pick(some_rest)], axis=1)

    some = shares_of(here // 2)
    for step in range(1, shards // 2):
        some = some + swap(shares_of((here // 2) ^ step), 2 * step)
    sum_attn_out, sum_router, sum_gain_f = (
        some[:, :width],
        some[:, width : width + experts],
        some[:, width + experts],
    )
    final = ordered(
        exchange_pieces(
            lambda w: jnp.concatenate(
                [
                    jnp.pad(
                        lax.dynamic_index_in_dim(wide, w, 0, keepdims=False),
                        ((0, 0), (0, width - 3 * part)),
                    ),
                    tail,
                ],
                axis=0,
            ),
            shards,
            here,
        ),
        here,
    )
    sum_attn_in = (
        jnp.stack([piece[:slim, : 3 * part] for piece in final], axis=1)
        .reshape(slim, shards, heads, 3, size)
        .transpose(0, 3, 1, 2, 4)
        .reshape(slim, 3 * width)
    )
    grad_rel_bias = jnp.concatenate(
        [
            piece[slim:].reshape(-1)[: heads * bucket_count].reshape(heads, bucket_count)
            for piece in final
        ],
        axis=0,
    ).T
    first = (owner * shards + here) * slim
    own_rows = (
        lax.dynamic_slice_in_dim(full_in, first, slim, 0)
        .reshape(slim, heads, shards, 3, size)
        .transpose(0, 3, 2, 1, 4)
        .reshape(slim, 3 * width)
    )
    sum_gain_a = jnp.sum(own_rows.astype(f32) * sum_attn_in, axis=1) / lax.dynamic_slice_in_dim(
        gain_a, first, slim, 0
    )
    return (
        mixed,
        grad_tokens,
        sum_gain_a,
        sum_attn_in,
        sum_attn_out,
        grad_rel_bias,
        sum_gain_f,
        sum_router,
        (in_kept + in_got.astype(f32))[None],
        (out_kept + out_got.astype(f32)).T[None],
    )


def solution(mesh):
    placed = (
        P(("expert", "wshard"), None),
        P("wshard"),
        P("wshard", None),
        P("wshard", None),
        P(),
        P(),
        P("wshard"),
        P("wshard", None),
        P(("expert", "wshard"), None),
        P("expert", None, None),
        P("expert", None, None),
        P(("expert", "wshard"), None),
    )
    return jax.shard_map(
        local,
        mesh=mesh,
        in_specs=placed,
        out_specs=(
            P(("expert", "wshard"), None),
            P(("expert", "wshard"), None),
            P(("expert", "wshard")),
            P(("expert", "wshard"), None),
            P(("expert", "wshard"), None),
            P(),
            P(("expert", "wshard")),
            P(("expert", "wshard"), None),
            P("expert", None, "wshard"),
            P("expert", "wshard", None),
        ),
        check_vma=False,
    )
```
